32 devices in a mesh: ctx: 8 (over y, x, core), tp: 4 (over z).
Axes of the slice: x: 2, y: 2, z: 4, core: 2. Of those that a mesh axis runs over, the one named last changes fastest.
Arguments:
- queries: bfloat16 [2048, 2048], P('ctx', 'tp'), may hold values from -6 to 6
- key_vectors: bfloat16 [2048, 2048], P('ctx', 'tp'), may hold values from -4 to 4
- value_vectors: bfloat16 [2048, 4096], P('ctx', 'tp'), may hold values from -6 to 6
- output_gate: bfloat16 [2048, 4096], P('ctx', 'tp'), may hold values from -6 to 6
- write_rate: float32 [2048, 32], P('ctx', 'tp'), may hold values from 0 to 1, as said below
- log_decay: float32 [2048, 32], P('ctx', 'tp'), may hold values from -1 to 0, as said below
- norm_gain: float32 [128], replicated, may hold values from 0.5 to 2
- out_weight: bfloat16 [4096, 2048], P('tp'), may hold values from -0.09375 to 0.09375
Outputs:
- mixed: bfloat16 [2048, 2048], P(('ctx', 'tp'))
The draws below stay inside these ranges and needn't reach their ends.
Inputs may be any that keep to these rules, and one draw needn't show every extreme that they name: `write_rate`: write strengths are positive. `log_decay`: log decays are negative.
All inputs are finite; a program needn't handle non-finite values.
Results may differ from the reference program's by a relative error of at most 0.025.
Values may be sent and summed in bfloat16 or wider, within the bound.
A program may use at most 64 MiB of HBM per device.

```python
import jax
import jax.numpy as jnp
from jax import lax

DK = 128
DV = 128
HK = 16
VALUE_HEAD_COUNT = 32
D = 2048
TOK_DEV = 256
SEQUENCE_TOKENS = 2048
N_TP = 4


def draw_key_vectors(key, part):
    key = jax.random.fold_in(key, 37)
    sequence_parts = jax.random.split(key, 2)
    sub_count = min(16, DK // 2)
    block_rows = 16
    block_count = SEQUENCE_TOKENS // block_rows
    head_keys = jax.random.split(sequence_parts[0], block_count * HK)
    orders = jax.vmap(lambda single: jax.random.permutation(single, DK))(head_keys)
    inside = (orders < sub_count).reshape(block_count, 1, HK * DK)
    weight_map = jnp.where(inside, 1.0, 0.4 * DK ** (-0.5)).astype(jnp.float32)
    weight_map = jnp.broadcast_to(weight_map, (block_count, block_rows, HK * DK)).reshape(SEQUENCE_TOKENS, HK * DK)
    raw_entries = jnp.clip(jax.random.normal(sequence_parts[1], (SEQUENCE_TOKENS, HK * DK), jnp.float32), -4.0, 4.0)
    return (raw_entries * weight_map).astype(jnp.bfloat16)


def draw_write_rate(key, part):
    key = jax.random.fold_in(key, 11)
    sequence_parts = jax.random.split(key, 2)
    levels = jnp.exp(jax.random.uniform(sequence_parts[0], (VALUE_HEAD_COUNT,), jnp.float32, -2.5, -1.05))
    jitter_factor = jax.random.uniform(sequence_parts[1], (SEQUENCE_TOKENS, VALUE_HEAD_COUNT), jnp.float32, 0.5, 1.5)
    return (levels[None, :] * jitter_factor).astype(jnp.float32)


def draw_log_decay(key, part):
    key = jax.random.fold_in(key, 23)
    sequence_parts = jax.random.split(key, 7)
    quick_share = 0.5
    jitter_factor = jax.random.uniform(sequence_parts[4], (SEQUENCE_TOKENS, VALUE_HEAD_COUNT), jnp.float32, 0.5, 1.5)
    quick_heads = jax.random.uniform(sequence_parts[0], (VALUE_HEAD_COUNT,), jnp.float32) < quick_share
    slow_rate = jax.random.uniform(sequence_parts[1], (VALUE_HEAD_COUNT,), jnp.float32, 0.05, 0.5) / SEQUENCE_TOKENS
    quick_rate = 1.0 / jax.random.uniform(sequence_parts[2], (VALUE_HEAD_COUNT,), jnp.float32, 30.0, 50.0)
    baseline = jnp.where(quick_heads, quick_rate, slow_rate)
    shard_scale = jnp.exp(jax.random.uniform(sequence_parts[3], (SEQUENCE_TOKENS // TOK_DEV, VALUE_HEAD_COUNT), jnp.float32, -0.7, 0.7))
    shard_scale = jnp.repeat(shard_scale, TOK_DEV, axis=0)
    spike_position = jax.random.randint(sequence_parts[5], (3,), 0, SEQUENCE_TOKENS)
    struck_value = jnp.any(jnp.arange(SEQUENCE_TOKENS)[:, None] == spike_position[None, :], axis=1)
    spike_penalty = jnp.log(jax.random.uniform(sequence_parts[6], (SEQUENCE_TOKENS, VALUE_HEAD_COUNT), jnp.float32, 0.55, 0.8))
    steady_decay = -baseline[None, :] * shard_scale * jitter_factor
    return (steady_decay + jnp.where(struck_value[:, None], spike_penalty, 0.0)).astype(jnp.float32)


def block_scale(key, extent, shards, least, largest):
    factor_of, own = 1.0, jax.random.fold_in(key, 6)
    for position, shards_of in shards:
        steps = jnp.exp(jax.random.uniform(jax.random.fold_in(own, position), (shards_of,), jnp.float32, least / len(shards), largest / len(shards)))
        factor_of = factor_of * jnp.repeat(steps, extent[position] // shards_of).reshape([-1 if axis == position else 1 for axis in range(len(extent))])
    return factor_of


def scatter_about(own_key, extent, deviation, reach, pieces=(), kind=jnp.bfloat16):
    drawn = jax.random.normal(own_key, extent, jnp.float32) * deviation
    if len(pieces) > 0:
        drawn = block_scale(own_key, extent, pieces, -0.22, 0.18) * drawn
    return jnp.clip(drawn, min=-reach, max=reach).astype(kind)


def setup_inputs(seed: int = 0) -> dict:
    splits = jax.random.split(jax.random.key(seed), 9)
    queries = scatter_about(splits[0], (SEQUENCE_TOKENS, HK * DK), 1.0, 6.0, ((0, 8), (1, 4)))
    key_vectors = draw_key_vectors(jax.random.fold_in(splits[8], 71), 0)
    value_vectors = scatter_about(splits[2], (SEQUENCE_TOKENS, VALUE_HEAD_COUNT * DV), 1.0, 6.0, ((0, 8), (1, 4)))
    output_gate = scatter_about(splits[3], (SEQUENCE_TOKENS, VALUE_HEAD_COUNT * DV), 1.0, 6.0, ((0, 8), (1, 4)))
    write_rate = draw_write_rate(jax.random.fold_in(splits[8], 71), 0)
    log_decay = draw_log_decay(jax.random.fold_in(splits[8], 71), 0)
    norm_gain = jnp.clip(jax.random.uniform(splits[6], (DV,), jnp.float32, 0.5, 2.0), 0.5, 2.0)
    out_weight = scatter_about(splits[7], (VALUE_HEAD_COUNT * DV, D), (VALUE_HEAD_COUNT * DV) ** -0.5, 0.09375, ((0, 4),))
    return {"queries": queries, "key_vectors": key_vectors, "value_vectors": value_vectors, "output_gate": output_gate, "write_rate": write_rate, "log_decay": log_decay, "norm_gain": norm_gain, "out_weight": out_weight}


highest_precision = lax.Precision.HIGHEST

def unit_vectors(source, count_heads, size_head):
    values_f = source.astype(jnp.float32).reshape(count_heads, size_head)
    return values_f * lax.rsqrt(lax.optimization_barrier(jnp.sum(values_f * values_f, axis=-1, keepdims=True)) + 1e-06)

def reference(queries, key_vectors, value_vectors, output_gate, write_rate, log_decay, norm_gain, out_weight):
    sharing = VALUE_HEAD_COUNT // HK

    def advance(carried_state, inputs):
        query_row, key_row, value_row, gate_row, rate_row, decay_row = inputs
        normalized_query = jnp.repeat(unit_vectors(query_row, HK, DK), sharing, axis=0)
        normalized_key = jnp.repeat(unit_vectors(key_row, HK, DK), sharing, axis=0)
        value_full = value_row.astype(jnp.float32).reshape(VALUE_HEAD_COUNT, DV)
        memory_readout = jnp.einsum('ns,nsd->nd', normalized_key, carried_state, precision=highest_precision)
        strength = rate_row[:, None, None]
        erased = carried_state - strength * normalized_key[:, :, None] * memory_readout[:, None, :]
        carried_state = jnp.exp(decay_row)[:, None, None] * erased + strength * normalized_key[:, :, None] * value_full[:, None, :]
        attention_core = jnp.einsum('ns,nsd->nd', normalized_query, carried_state, precision=highest_precision)
        square_mean = lax.optimization_barrier(jnp.mean(attention_core * attention_core, axis=-1, keepdims=True))
        gate_full = gate_row.astype(jnp.float32).reshape(VALUE_HEAD_COUNT, DV)
        normed = attention_core * lax.rsqrt(square_mean + 1e-06) * norm_gain * jax.nn.silu(gate_full)
        return (carried_state, normed.reshape(VALUE_HEAD_COUNT * DV).astype(jnp.bfloat16))
    initial = jnp.zeros((VALUE_HEAD_COUNT, DK, DV), jnp.float32)
    _, normed_all = lax.scan(advance, initial, (queries, key_vectors, value_vectors, output_gate, write_rate, log_decay))
    group_width = VALUE_HEAD_COUNT * DV // N_TP
    total = jnp.zeros((SEQUENCE_TOKENS, D), jnp.float32)
    for group_index in range(N_TP):
        lower_edge = group_index * group_width
        part_sum = jnp.dot(normed_all[:, lower_edge:lower_edge + group_width], out_weight[lower_edge:lower_edge + group_width], preferred_element_type=jnp.float32).astype(jnp.bfloat16)
        part_sum = lax.optimization_barrier(part_sum)
        total = total + part_sum.astype(jnp.float32)
    return total.astype(jnp.bfloat16)
```

```python
import functools

import jax
import jax.numpy as jnp
from jax import lax
from jax.experimental import pallas as pl
from jax.experimental.pallas import tpu as pltpu
from jax.sharding import PartitionSpec as P

DK = 128
DV = 128
MESH = pl.DeviceIdType.MESH
f32, bf16 = jnp.float32, jnp.bfloat16


def mm(left, right):
    return jnp.dot(left, right, preferred_element_type=f32)


def mm_rows(left, right):
    return lax.dot_general(left, right, (((1,), (1,)), ((), ())), preferred_element_type=f32)


def mm_cols(left, right):
    return lax.dot_general(left, right, (((0,), (0,)), ((), ())), preferred_element_type=f32)


def unit_lower_inverse(lower, row, col):
    size = lower.shape[0]
    eye = row == col

    def between(step):
        return (row // (2 * step) == col // (2 * step)) & (row // step != col // step)

    inverse = jnp.where(eye, 1.0, jnp.where(between(1), -lower, 0.0))
    step = 2
    while step < size:
        coupling = jnp.where(between(step), lower, 0.0).astype(bf16)
        rounded = inverse.astype(bf16)
        inverse = inverse - mm(rounded, mm(coupling, rounded).astype(bf16))
        step *= 2
    rounded = inverse.astype(bf16)
    high = lower.astype(bf16)
    low = (lower - high.astype(f32)).astype(bf16)
    base = rounded.astype(f32)
    residual = jnp.where(eye, 1.0, 0.0) - base - mm(high, rounded) - mm(low, rounded)
    return base + mm(rounded, residual.astype(bf16))


def summary_kernel(sharing, q_ref, k_ref, v_ref, rate_ref, decay_ref, map_ref, read_ref, own_ref):
    group = pl.program_id(0)
    tokens = q_ref.shape[0]
    half = tokens // 2
    row = lax.broadcasted_iota(jnp.int32, (tokens, tokens), 0)
    col = lax.broadcasted_iota(jnp.int32, (tokens, tokens), 1)
    eye, inclusive, strict = row == col, row >= col, row > col
    half_row = lax.broadcasted_iota(jnp.int32, (half, half), 0)
    half_col = lax.broadcasted_iota(jnp.int32, (half, half), 1)
    key_row = lax.broadcasted_iota(jnp.int32, (DK, DK), 0)
    key_col = lax.broadcasted_iota(jnp.int32, (DK, DK), 1)
    lane = lax.broadcasted_iota(jnp.int32, rate_ref.shape, 1)

    def to_row(column):
        return jnp.sum(jnp.where(eye, column, 0.0), axis=0, keepdims=True)

    def to_col(line):
        return jnp.sum(jnp.where(eye, line, 0.0), axis=1, keepdims=True)

    queries, keys = q_ref[...], k_ref[...]
    queries_f, keys_f = queries.astype(f32), keys.astype(f32)
    query_scale = lax.rsqrt(jnp.sum(queries_f * queries_f, axis=1, keepdims=True) + 1e-06)
    key_scale = lax.rsqrt(jnp.sum(keys_f * keys_f, axis=1, keepdims=True) + 1e-06)
    key_scale_row = to_row(key_scale)
    gram = mm_rows(keys, keys) * key_scale
    reads = mm_rows(queries, keys) * query_scale
    scaled_queries = queries_f * query_scale

    for member in range(sharing):
        head = group * sharing + member
        here = lane == head
        rate = jnp.sum(jnp.where(here, rate_ref[...], 0.0), axis=1, keepdims=True)
        decay = jnp.sum(jnp.where(here, decay_ref[...], 0.0), axis=1, keepdims=True)
        total_row = jnp.sum(jnp.where(row <= col, decay, 0.0), axis=0, keepdims=True)
        total = to_col(total_row)
        rate_row = to_row(rate)
        erase_row = rate_row * jnp.exp(total_row) * key_scale_row
        ratios = jnp.where(inclusive, jnp.exp(jnp.where(inclusive, total - total_row, 0.0)), 0.0)
        ratios = ratios * key_scale_row
        scores = (reads * ratios).astype(bf16)
        lower = jnp.where(strict, rate * gram * ratios, 0.0)
        first = unit_lower_inverse(lower[:half, :half], half_row, half_col)
        second = unit_lower_inverse(lower[half:, half:], half_row, half_col)
        across = mm(lower[half:, :half].astype(bf16), first.astype(bf16))
        across = -mm(second.astype(bf16), across.astype(bf16))
        values = v_ref[:, member * DV : (member + 1) * DV]

        def solved(scale_row, right):
            left_scale, right_scale = scale_row[:, :half], scale_row[:, half:]
            top = mm((first * left_scale).astype(bf16), right[:half])
            bottom = mm((across * left_scale).astype(bf16), right[:half])
            bottom += mm((second * right_scale).astype(bf16), right[half:])
            return jnp.concatenate([top, bottom], axis=0)

        both = jnp.concatenate([solved(erase_row, keys), solved(rate_row, values)], axis=1)
        closing = total[tokens - 1 :, :]
        weight = jnp.exp(closing - total) * key_scale
        summary = mm_cols(keys, (both * weight).astype(bf16))
        fade = jnp.exp(closing)
        moved = jnp.where(key_row == key_col, fade, 0.0) - summary[:, :DK]
        map_ref[member, :, :DK] = moved.astype(bf16)
        map_ref[member, :, DK:] = summary[:, DK:].astype(bf16)
        seen = mm(scores, both.astype(bf16))
        place = slice(member * DV, (member + 1) * DV)
        read_ref[:, place] = (jnp.exp(total) * scaled_queries - seen[:, :DK]).astype(bf16)
        own_ref[:, place] = seen[:, DK:]


def finish_kernel(
    n, groups, map_ref, read_ref, own_ref, gate_ref, gain_ref, weight_hbm, out_ref,
    arrived, leaving, state, normed, weight, part, out_r, out_l, in_r, in_l,
    weight_sem, map_send, map_recv, state_send, state_recv,
    send_r, recv_r, send_l, recv_l,
):
    heads = map_ref.shape[0]
    apart = n // heads
    chunks, _, rows, width = part.shape
    me, spot = lax.axis_index("ctx"), lax.axis_index("tp")
    my_head = me // apart
    owner = lax.rem(me, apart) == 0

    weight_copy = pltpu.make_async_copy(weight_hbm, weight, weight_sem)
    weight_copy.start()

    barrier = pltpu.get_barrier_semaphore()
    for other in range(n):
        @pl.when(me != other)
        def _():
            pl.semaphore_signal(barrier, inc=1, device_id={"ctx": other}, device_id_type=MESH)

    after, before = lax.rem(spot + 1, groups), lax.rem(spot + groups - 1, groups)

    @pl.when(spot > 0)
    def _():
        pl.semaphore_signal(barrier, inc=1, device_id={"tp": before}, device_id_type=MESH)

    @pl.when(spot < groups - 1)
    def _():
        pl.semaphore_signal(barrier, inc=1, device_id={"tp": after}, device_id_type=MESH)

    peers = (spot > 0).astype(jnp.int32) + (spot < groups - 1).astype(jnp.int32)
    pl.semaphore_wait(barrier, n - 1 + peers)

    def map_copy(head, slot, target):
        return pltpu.make_async_remote_copy(
            src_ref=map_ref.at[head], dst_ref=arrived.at[slot],
            send_sem=map_send.at[head], recv_sem=map_recv.at[slot],
            device_id={"ctx": target}, device_id_type=MESH,
        )

    for head in range(heads):
        @pl.when((me != head * apart) & (me < n - 1))
        def _():
            map_copy(head, me, head * apart).start()

    def state_copy(head, target):
        return pltpu.make_async_remote_copy(
            src_ref=leaving.at[target], dst_ref=state.at[head],
            send_sem=state_send.at[target], recv_sem=state_recv.at[head],
            device_id={"ctx": target}, device_id_type=MESH,
        )

    @pl.when(me == 0)
    def _():
        state[...] = jnp.zeros_like(state)

    @pl.when(owner)
    def _():
        arrived[pl.ds(me, 1)] = map_ref[pl.ds(my_head, 1)]
        current = jnp.zeros((DK, DV), f32)
        for step in range(n - 1):
            @pl.when(me != step)
            def _():
                map_copy(0, step, step).wait_recv()

            high = current.astype(bf16)
            low = (current - high.astype(f32)).astype(bf16)
            turned = mm(arrived[step, :, :DK], jnp.concatenate([high, low], axis=1))
            current = turned[:, :DV] + turned[:, DV:] + arrived[step, :, DK:].astype(f32)

            @pl.when(me != step + 1)
            def _():
                leaving[step + 1] = current.astype(bf16)
                state_copy(my_head, step + 1).start()

            @pl.when(me == step + 1)
            def _():
                state[pl.ds(my_head, 1)] = current.astype(bf16)[None]

    gain = gain_ref[...]
    for head in range(heads):
        @pl.when((me > 0) & (me != head * apart))
        def _():
            state_copy(head, 0).wait_recv()

        place = slice(head * DV, (head + 1) * DV)
        core = mm(read_ref[:, place], state[head]) + own_ref[:, place]
        square_mean = jnp.mean(core * core, axis=1, keepdims=True)
        gate = gate_ref[:, place].astype(f32)
        gated = core * lax.rsqrt(square_mean + 1e-06) * gain * (gate / (1.0 + jnp.exp(-gate)))
        normed[:, place] = gated.astype(bf16)

    def right_copy(source, c, target):
        return pltpu.make_async_remote_copy(
            src_ref=source.at[c, target], dst_ref=in_r.at[c, target],
            send_sem=send_r.at[c, target], recv_sem=recv_r.at[c, target],
            device_id={"tp": after}, device_id_type=MESH,
        )

    def left_copy(source, c, target):
        return pltpu.make_async_remote_copy(
            src_ref=source.at[c, target], dst_ref=in_l.at[c, target],
            send_sem=send_l.at[c, target], recv_sem=recv_l.at[c, target],
            device_id={"tp": before}, device_id_type=MESH,
        )

    @pl.when(spot == 0)
    def _():
        in_r[:, 0] = jnp.zeros_like(in_r[:, 0])

    @pl.when(spot == groups - 1)
    def _():
        in_l[:, groups - 1] = jnp.zeros_like(in_l[:, groups - 1])

    weight_copy.wait()
    for c in range(chunks):
        product = mm(normed[...], weight[:, c * width : (c + 1) * width]).astype(bf16)
        part[c] = product.reshape(groups, rows, width)

        @pl.when(spot == 0)
        def _():
            for target in range(groups - 1, 0, -1):
                right_copy(part, c, target).start()

        @pl.when(spot == groups - 1)
        def _():
            for target in range(groups - 1):
                left_copy(part, c, target).start()

    for c in range(chunks):
        def relay(step, carry):
            far = groups - 1 - step

            @pl.when((spot > 0) & (far > spot))
            def _():
                right_copy(part, c, far).wait_recv()
                out_r[c, far] = (in_r[c, far].astype(f32) + part[c, far].astype(f32)).astype(bf16)
                right_copy(out_r, c, far).start()

            @pl.when((spot < groups - 1) & (step < spot))
            def _():
                left_copy(part, c, step).wait_recv()
                out_l[c, step] = (in_l[c, step].astype(f32) + part[c, step].astype(f32)).astype(bf16)
                left_copy(out_l, c, step).start()

            return carry

        lax.fori_loop(0, groups - 1, relay, 0)

    for c in range(chunks):
        @pl.when(spot > 0)
        def _():
            right_copy(part, c, spot).wait_recv()

        @pl.when(spot < groups - 1)
        def _():
            left_copy(part, c, spot).wait_recv()

        mixed = part[c, spot].astype(f32) + in_r[c, spot].astype(f32) + in_l[c, spot].astype(f32)
        out_ref[:, c * width : (c + 1) * width] = mixed.astype(bf16)

    for head in range(heads):
        @pl.when((me != head * apart) & (me < n - 1))
        def _():
            map_copy(head, me, head * apart).wait_send()

    for target in range(1, n):
        @pl.when(owner & (me != target))
        def _():
            state_copy(my_head, target).wait_send()

    for c in range(chunks):
        def drain(target, carry):
            @pl.when(target > spot)
            def _():
                right_copy(part, c, target).wait_send()

            @pl.when(target < spot)
            def _():
                left_copy(part, c, target).wait_send()

            return carry

        lax.fori_loop(0, groups, drain, 0)


def local(n, groups, queries, key_vectors, value_vectors, output_gate, write_rate, log_decay, norm_gain, out_weight):
    tokens = queries.shape[0]
    key_heads = queries.shape[1] // DK
    heads = value_vectors.shape[1] // DV
    sharing = heads // key_heads
    features, model = out_weight.shape
    small = pl.BlockSpec((tokens, heads), lambda g: (0, 0))
    maps, read, own = pl.pallas_call(
        functools.partial(summary_kernel, sharing),
        grid=(key_heads,),
        in_specs=[
            pl.BlockSpec((tokens, DK), lambda g: (0, g)),
            pl.BlockSpec((tokens, DK), lambda g: (0, g)),
            pl.BlockSpec((tokens, sharing * DV), lambda g: (0, g)),
            small,
            small,
        ],
        out_specs=[
            pl.BlockSpec((sharing, DK, DK + DV), lambda g: (g, 0, 0)),
            pl.BlockSpec((tokens, sharing * DV), lambda g: (0, g)),
            pl.BlockSpec((tokens, sharing * DV), lambda g: (0, g)),
        ],
        out_shape=[
            jax.ShapeDtypeStruct((heads, DK, DK + DV), bf16),
            jax.ShapeDtypeStruct((tokens, heads * DV), bf16),
            jax.ShapeDtypeStruct((tokens, heads * DV), f32),
        ],
        compiler_params=pltpu.CompilerParams(vmem_limit_bytes=32 * 2**20),
    )(queries, key_vectors, value_vectors, write_rate, log_decay)

    rows = tokens // groups
    chunks = 4
    width = model // chunks
    piece = pltpu.VMEM((chunks, groups, rows, width), bf16)
    dma = pltpu.SemaphoreType.DMA
    vmem = pl.BlockSpec(memory_space=pltpu.VMEM)
    return pl.pallas_call(
        functools.partial(finish_kernel, n, groups),
        in_specs=[vmem] * 5 + [pl.BlockSpec(memory_space=pl.ANY)],
        out_specs=vmem,
        out_shape=jax.ShapeDtypeStruct((rows, model), bf16),
        scratch_shapes=[
            pltpu.VMEM((n, DK, DK + DV), bf16),
            pltpu.VMEM((n, DK, DV), bf16),
            pltpu.VMEM((heads, DK, DV), bf16),
            pltpu.VMEM((tokens, features), bf16),
            pltpu.VMEM((features, model), bf16),
            piece, piece, piece, piece, piece,
            dma, dma((heads,)), dma((n,)), dma((n,)), dma((heads,)),
            dma((chunks, groups)), dma((chunks, groups)), dma((chunks, groups)), dma((chunks, groups)),
        ],
        compiler_params=pltpu.CompilerParams(
            collective_id=0, has_side_effects=True, vmem_limit_bytes=48 * 2**20
        ),
    )(maps, read, own, output_gate, norm_gain.reshape(1, DV), out_weight)


def solution(mesh):
    placed = (
        P("ctx", "tp"),
        P("ctx", "tp"),
        P("ctx", "tp"),
        P("ctx", "tp"),
        P("ctx", "tp"),
        P("ctx", "tp"),
        P(),
        P("tp", None),
    )
    body = functools.partial(local, mesh.shape["ctx"], mesh.shape["tp"])
    return jax.shard_map(
        body, mesh=mesh, in_specs=placed, out_specs=P(("ctx", "tp"), None), check_vma=False
    )
```

```python
import functools

import jax
import jax.numpy as jnp
from jax import lax
from jax.experimental import pallas as pl
from jax.experimental.pallas import tpu as pltpu
from jax.sharding import PartitionSpec as P

DK = 128
DV = 128
MESH = pl.DeviceIdType.MESH
f32, bf16 = jnp.float32, jnp.bfloat16


def mm(left, right):
    return jnp.dot(left, right, preferred_element_type=f32)


def mm_rows(left, right):
    return lax.dot_general(left, right, (((1,), (1,)), ((), ())), preferred_element_type=f32)


def mm_cols(left, right):
    return lax.dot_general(left, right, (((0,), (0,)), ((), ())), preferred_element_type=f32)


def unit_lower_inverses(lowers):
    size = lowers[0].shape[0]
    row = lax.broadcasted_iota(jnp.int32, (size, size), 0)
    col = lax.broadcasted_iota(jnp.int32, (size, size), 1)
    apart = row ^ col
    eye = jnp.where(row == col, 1.0, 0.0)
    inverses = [eye - jnp.where(apart == 1, lower, 0.0) for lower in lowers]
    step = 2
    while step < size:
        coupling = (apart >= step) & (apart < 2 * step)
        rounded = [inverse.astype(bf16) for inverse in inverses]
        inner = [
            mm(jnp.where(coupling, lower, 0.0).astype(bf16), r).astype(bf16)
            for lower, r in zip(lowers, rounded)
        ]
        inverses = [inverse - mm(r, i) for inverse, r, i in zip(inverses, rounded, inner)]
        step *= 2
    rounded = [inverse.astype(bf16) for inverse in inverses]
    highs = [lower.astype(bf16) for lower in lowers]
    lows = [(lower - high.astype(f32)).astype(bf16) for lower, high in zip(lowers, highs)]
    residuals = [
        (eye - r.astype(f32) - mm(high, r) - mm(low, r)).astype(bf16)
        for high, low, r in zip(highs, lows, rounded)
    ]
    return [r.astype(f32) + mm(r, residual) for r, residual in zip(rounded, residuals)]


def summarize(groups, sharing, q_ref, k_ref, v_ref, rate_ref, decay_ref, map_ref, read_ref, own_ref):
    tokens = q_ref.shape[0]
    half = tokens // 2
    row = lax.broadcasted_iota(jnp.int32, (tokens, tokens), 0)
    col = lax.broadcasted_iota(jnp.int32, (tokens, tokens), 1)
    eye, inclusive, strict = row == col, row >= col, row > col
    key_row = lax.broadcasted_iota(jnp.int32, (DK, DK), 0)
    key_col = lax.broadcasted_iota(jnp.int32, (DK, DK), 1)

    def to_row(column):
        return jnp.sum(jnp.where(eye, column, 0.0), axis=0, keepdims=True)

    def to_col(line):
        return jnp.sum(jnp.where(eye, line, 0.0), axis=1, keepdims=True)

    parts = []
    for group in groups:
        key_place = slice(group * DK, (group + 1) * DK)
        queries, keys = q_ref[:, key_place], k_ref[:, key_place]
        queries_f, keys_f = queries.astype(f32), keys.astype(f32)
        query_scale = lax.rsqrt(jnp.sum(queries_f * queries_f, axis=1, keepdims=True) + 1e-06)
        key_scale = lax.rsqrt(jnp.sum(keys_f * keys_f, axis=1, keepdims=True) + 1e-06)
        key_scale_row = to_row(key_scale)
        gram = mm_rows(keys, keys) * key_scale
        reads = mm_rows(queries, keys) * query_scale
        for member in range(sharing):
            head = group * sharing + member
            rate_row = rate_ref[head : head + 1, :]
            decay_row = decay_ref[head : head + 1, :]
            rate, decay = to_col(rate_row), to_col(decay_row)
            total_row = jnp.sum(jnp.where(row <= col, decay, 0.0), axis=0, keepdims=True)
            total = to_col(total_row)
            erase_row = rate_row * jnp.exp(total_row) * key_scale_row
            ratios = jnp.where(inclusive, jnp.exp(jnp.where(inclusive, total - total_row, 0.0)), 0.0)
            ratios = ratios * key_scale_row
            scores = (reads * ratios).astype(bf16)
            lower = jnp.where(strict, rate * gram * ratios, 0.0)
            read = jnp.exp(total) * query_scale * queries_f
            parts.append((head, keys, key_scale, rate_row, erase_row, total, scores, lower, read))

    inverses = unit_lower_inverses(
        [block for part in parts for block in (part[7][:half, :half], part[7][half:, half:])]
    )
    firsts, seconds = inverses[0::2], inverses[1::2]
    inner = [
        mm(part[7][half:, :half].astype(bf16), first.astype(bf16)).astype(bf16)
        for part, first in zip(parts, firsts)
    ]
    corners = [-mm(second.astype(bf16), i) for second, i in zip(seconds, inner)]

    for part, first, second, corner in zip(parts, firsts, seconds, corners):
        head, keys, key_scale, rate_row, erase_row, total, scores, _, read = part
        place = slice(head * DV, (head + 1) * DV)

        def solved(scale_row, right):
            left_scale, right_scale = scale_row[:, :half], scale_row[:, half:]
            top = mm((first * left_scale).astype(bf16), right[:half])
            bottom = mm((corner * left_scale).astype(bf16), right[:half])
            bottom += mm((second * right_scale).astype(bf16), right[half:])
            return jnp.concatenate([top, bottom], axis=0)

        both = jnp.concatenate([solved(erase_row, keys), solved(rate_row, v_ref[:, place])], axis=1)
        closing = total[tokens - 1 :, :]
        weight = jnp.exp(closing - total) * key_scale
        summary = mm_cols(keys, (both * weight).astype(bf16))
        moved = jnp.where(key_row == key_col, jnp.exp(closing), 0.0) - summary[:, :DK]
        map_ref[head, :, :DK] = moved.astype(bf16)
        map_ref[head, :, DK:] = summary[:, DK:].astype(bf16)
        seen = mm(scores, both.astype(bf16))
        read_ref[:, place] = (read - seen[:, :DK]).astype(bf16)
        own_ref[:, place] = seen[:, DK:]


def layer_kernel(
    n, groups, q_hbm, k_hbm, v_hbm, gate_hbm, rate_hbm, decay_hbm, gain_hbm, weight_hbm, out_ref,
    q_ref, k_ref, v_ref, gate_ref, rate_ref, decay_ref, gain_ref, weight,
    map_ref, read_ref, own_ref, gating,
    arrived, leaving, state, normed, part, out_r, out_l, in_r, in_l,
    load_sem, map_send, map_recv, state_send, state_recv,
    send_r, recv_r, send_l, recv_l,
):
    heads = map_ref.shape[0]
    apart = n // heads
    chunks, _, rows, width = part.shape
    me, spot = lax.axis_index("ctx"), lax.axis_index("tp")
    my_head = me // apart
    owner = lax.rem(me, apart) == 0

    loads = [
        pltpu.make_async_copy(source, target, load_sem.at[i])
        for i, (source, target) in enumerate((
            (k_hbm, k_ref), (q_hbm, q_ref), (rate_hbm, rate_ref), (decay_hbm, decay_ref),
            (v_hbm, v_ref), (gain_hbm, gain_ref), (gate_hbm, gate_ref), (weight_hbm, weight),
        ))
    ]
    for load in loads:
        load.start()

    barrier = pltpu.get_barrier_semaphore()
    for other in range(n):
        @pl.when(me != other)
        def _():
            pl.semaphore_signal(barrier, inc=1, device_id={"ctx": other}, device_id_type=MESH)

    after, before = lax.rem(spot + 1, groups), lax.rem(spot + groups - 1, groups)

    @pl.when(spot > 0)
    def _():
        pl.semaphore_signal(barrier, inc=1, device_id={"tp": before}, device_id_type=MESH)

    @pl.when(spot < groups - 1)
    def _():
        pl.semaphore_signal(barrier, inc=1, device_id={"tp": after}, device_id_type=MESH)

    peers = (spot > 0).astype(jnp.int32) + (spot < groups - 1).astype(jnp.int32)
    def map_copy(head, slot, target):
        return pltpu.make_async_remote_copy(
            src_ref=map_ref.at[head], dst_ref=arrived.at[slot],
            send_sem=map_send.at[head], recv_sem=map_recv.at[slot],
            device_id={"ctx": target}, device_id_type=MESH,
        )

    key_heads = k_ref.shape[1] // DK
    sharing = heads // key_heads
    batch = min(2, key_heads)
    for load in loads[:5]:
        load.wait()

    for start in range(0, key_heads, batch):
        summarize(
            range(start, start + batch), sharing,
            q_ref, k_ref, v_ref, rate_ref, decay_ref, map_ref, read_ref, own_ref,
        )
        if start == 0:
            pl.semaphore_wait(barrier, n - 1 + peers)
        for head in range(start * sharing, (start + batch) * sharing):
            @pl.when((me != head * apart) & (me < n - 1))
            def _():
                map_copy(head, me, head * apart).start()

    for load in loads[5:]:
        load.wait()
    gain = gain_ref[...]
    for head in range(heads):
        place = slice(head * DV, (head + 1) * DV)
        gate = gate_ref[:, place].astype(f32)
        gating[:, place] = gain * (gate / (1.0 + jnp.exp(-gate)))

    def state_copy(head, target):
        return pltpu.make_async_remote_copy(
            src_ref=leaving.at[target], dst_ref=state.at[head],
            send_sem=state_send.at[target], recv_sem=state_recv.at[head],
            device_id={"ctx": target}, device_id_type=MESH,
        )

    @pl.when(me == 0)
    def _():
        state[...] = jnp.zeros_like(state)

    @pl.when(owner)
    def _():
        arrived[pl.ds(me, 1)] = map_ref[pl.ds(my_head, 1)]
        current = jnp.zeros((DK, DV), f32)
        for step in range(n - 1):
            @pl.when(me != step)
            def _():
                map_copy(0, step, step).wait_recv()

            high = current.astype(bf16)
            low = (current - high.astype(f32)).astype(bf16)
            turned = mm(arrived[step, :, :DK], jnp.concatenate([high, low], axis=1))
            current = turned[:, :DV] + turned[:, DV:] + arrived[step, :, DK:].astype(f32)

            @pl.when(me != step + 1)
            def _():
                leaving[step + 1] = current.astype(bf16)
                state_copy(my_head, step + 1).start()

            @pl.when(me == step + 1)
            def _():
                state[pl.ds(my_head, 1)] = current.astype(bf16)[None]

    for head in range(heads):
        @pl.when((me > 0) & (me != head * apart))
        def _():
            state_copy(head, 0).wait_recv()

        place = slice(head * DV, (head + 1) * DV)
        core = mm(read_ref[:, place], state[head]) + own_ref[:, place]
        square_mean = jnp.mean(core * core, axis=1, keepdims=True)
        normed[:, place] = (core * lax.rsqrt(square_mean + 1e-06) * gating[:, place]).astype(bf16)

    def right_copy(source, c, target):
        return pltpu.make_async_remote_copy(
            src_ref=source.at[c, target], dst_ref=in_r.at[c, target],
            send_sem=send_r.at[c, target], recv_sem=recv_r.at[c, target],
            device_id={"tp": after}, device_id_type=MESH,
        )

    def left_copy(source, c, target):
        return pltpu.make_async_remote_copy(
            src_ref=source.at[c, target], dst_ref=in_l.at[c, target],
            send_sem=send_l.at[c, target], recv_sem=recv_l.at[c, target],
            device_id={"tp": before}, device_id_type=MESH,
        )

    @pl.when(spot == 0)
    def _():
        in_r[:, 0] = jnp.zeros_like(in_r[:, 0])

    @pl.when(spot == groups - 1)
    def _():
        in_l[:, groups - 1] = jnp.zeros_like(in_l[:, groups - 1])

    for c in range(chunks):
        product = mm(normed[...], weight[:, c * width : (c + 1) * width]).astype(bf16)
        part[c] = product.reshape(groups, rows, width)

        @pl.when(spot == 0)
        def _():
            for target in range(groups - 1, 0, -1):
                right_copy(part, c, target).start()

        @pl.when(spot == groups - 1)
        def _():
            for target in range(groups - 1):
                left_copy(part, c, target).start()

    for c in range(chunks):
        def relay(step, carry):
            far = groups - 1 - step

            @pl.when((spot > 0) & (far > spot))
            def _():
                right_copy(part, c, far).wait_recv()
                out_r[c, far] = (in_r[c, far].astype(f32) + part[c, far].astype(f32)).astype(bf16)
                right_copy(out_r, c, far).start()

            @pl.when((spot < groups - 1) & (step < spot))
            def _():
                left_copy(part, c, step).wait_recv()
                out_l[c, step] = (in_l[c, step].astype(f32) + part[c, step].astype(f32)).astype(bf16)
                left_copy(out_l, c, step).start()

            return carry

        lax.fori_loop(0, groups - 1, relay, 0)

    for c in range(chunks):
        @pl.when(spot > 0)
        def _():
            right_copy(part, c, spot).wait_recv()

        @pl.when(spot < groups - 1)
        def _():
            left_copy(part, c, spot).wait_recv()

        mixed = part[c, spot].astype(f32) + in_r[c, spot].astype(f32) + in_l[c, spot].astype(f32)
        out_ref[:, c * width : (c + 1) * width] = mixed.astype(bf16)

    for head in range(heads):
        @pl.when((me != head * apart) & (me < n - 1))
        def _():
            map_copy(head, me, head * apart).wait_send()

    for target in range(1, n):
        @pl.when(owner & (me != target))
        def _():
            state_copy(my_head, target).wait_send()

    for c in range(chunks):
        def drain(target, carry):
            @pl.when(target > spot)
            def _():
                right_copy(part, c, target).wait_send()

            @pl.when(target < spot)
            def _():
                left_copy(part, c, target).wait_send()

            return carry

        lax.fori_loop(0, groups, drain, 0)


def local(n, groups, queries, key_vectors, value_vectors, output_gate, write_rate, log_decay, norm_gain, out_weight):
    tokens = queries.shape[0]
    heads = value_vectors.shape[1] // DV
    features, model = out_weight.shape
    rows = tokens // groups
    chunks = 4
    width = model // chunks
    piece = pltpu.VMEM((chunks, groups, rows, width), bf16)
    dma = pltpu.SemaphoreType.DMA
    inputs = (
        queries, key_vectors, value_vectors, output_gate,
        write_rate.T, log_decay.T, norm_gain.reshape(1, DV), out_weight,
    )
    return pl.pallas_call(
        functools.partial(layer_kernel, n, groups),
        in_specs=[pl.BlockSpec(memory_space=pl.ANY)] * len(inputs),
        out_specs=pl.BlockSpec(memory_space=pltpu.VMEM),
        out_shape=jax.ShapeDtypeStruct((rows, model), bf16),
        scratch_shapes=[pltpu.VMEM(array.shape, array.dtype) for array in inputs] + [
            pltpu.VMEM((heads, DK, DK + DV), bf16),
            pltpu.VMEM((tokens, features), bf16),
            pltpu.VMEM((tokens, features), f32),
            pltpu.VMEM((tokens, features), f32),
            pltpu.VMEM((n, DK, DK + DV), bf16),
            pltpu.VMEM((n, DK, DV), bf16),
            pltpu.VMEM((heads, DK, DV), bf16),
            pltpu.VMEM((tokens, features), bf16),
            piece, piece, piece, piece, piece,
            dma((len(inputs),)), dma((heads,)), dma((n,)), dma((n,)), dma((heads,)),
            dma((chunks, groups)), dma((chunks, groups)), dma((chunks, groups)), dma((chunks, groups)),
        ],
        compiler_params=pltpu.CompilerParams(
            collective_id=0, has_side_effects=True, vmem_limit_bytes=56 * 2**20
        ),
    )(*inputs)


def solution(mesh):
    placed = (
        P("ctx", "tp"),
        P("ctx", "tp"),
        P("ctx", "tp"),
        P("ctx", "tp"),
        P("ctx", "tp"),
        P("ctx", "tp"),
        P(),
        P("tp", None),
    )
    body = functools.partial(local, mesh.shape["ctx"], mesh.shape["tp"])
    return jax.shard_map(
        body, mesh=mesh, in_specs=placed, out_specs=P(("ctx", "tp"), None), check_vma=False
    )
```

```python
import functools

import jax
import jax.numpy as jnp
from jax import lax
from jax.experimental import pallas as pl
from jax.experimental.pallas import tpu as pltpu
from jax.sharding import PartitionSpec as P

DK = 128
DV = 128
MESH = pl.DeviceIdType.MESH
f32, bf16 = jnp.float32, jnp.bfloat16


def mm(left, right):
    return jnp.dot(left, right, preferred_element_type=f32)


def mm_rows(left, right):
    return lax.dot_general(left, right, (((1,), (1,)), ((), ())), preferred_element_type=f32)


def mm_cols(left, right):
    return lax.dot_general(left, right, (((0,), (0,)), ((), ())), preferred_element_type=f32)


def unit_lower_inverses(lowers):
    size = lowers[0].shape[0]
    row = lax.broadcasted_iota(jnp.int32, (size, size), 0)
    col = lax.broadcasted_iota(jnp.int32, (size, size), 1)
    apart = row ^ col
    eye = jnp.where(row == col, 1.0, 0.0)
    inverses = [eye - jnp.where(apart == 1, lower, 0.0) for lower in lowers]
    step = 2
    while step < size:
        coupling = (apart >= step) & (apart < 2 * step)
        rounded = [inverse.astype(bf16) for inverse in inverses]
        inner = [
            mm(jnp.where(coupling, lower, 0.0).astype(bf16), r).astype(bf16)
            for lower, r in zip(lowers, rounded)
        ]
        inverses = [inverse - mm(r, i) for inverse, r, i in zip(inverses, rounded, inner)]
        step *= 2
    rounded = [inverse.astype(bf16) for inverse in inverses]
    highs = [lower.astype(bf16) for lower in lowers]
    lows = [(lower - high.astype(f32)).astype(bf16) for lower, high in zip(lowers, highs)]
    residuals = [
        (eye - r.astype(f32) - mm(high, r) - mm(low, r)).astype(bf16)
        for high, low, r in zip(highs, lows, rounded)
    ]
    return [r.astype(f32) + mm(r, residual) for r, residual in zip(rounded, residuals)]


def prepare(key_heads, sharing, q_ref, k_ref, rate_ref, decay_ref, scores_ref):
    tokens = q_ref.shape[0]
    row = lax.broadcasted_iota(jnp.int32, (tokens, tokens), 0)
    col = lax.broadcasted_iota(jnp.int32, (tokens, tokens), 1)
    eye, inclusive, strict = row == col, row >= col, row > col

    def to_row(column):
        return jnp.sum(jnp.where(eye, column, 0.0), axis=0, keepdims=True)

    def to_col(line):
        return jnp.sum(jnp.where(eye, line, 0.0), axis=1, keepdims=True)

    parts = []
    for group in range(key_heads):
        key_place = slice(group * DK, (group + 1) * DK)
        queries, keys = q_ref[:, key_place], k_ref[:, key_place]
        queries_f, keys_f = queries.astype(f32), keys.astype(f32)
        query_scale = lax.rsqrt(jnp.sum(queries_f * queries_f, axis=1, keepdims=True) + 1e-06)
        key_scale = lax.rsqrt(jnp.sum(keys_f * keys_f, axis=1, keepdims=True) + 1e-06)
        key_scale_row = to_row(key_scale)
        gram = mm_rows(keys, keys) * key_scale
        reads = mm_rows(queries, keys) * query_scale
        for member in range(sharing):
            head = group * sharing + member
            rate_row = rate_ref[head : head + 1, :]
            decay_row = decay_ref[head : head + 1, :]
            rate, decay = to_col(rate_row), to_col(decay_row)
            total_row = jnp.sum(jnp.where(row <= col, decay, 0.0), axis=0, keepdims=True)
            total = to_col(total_row)
            erase_row = rate_row * jnp.exp(total_row) * key_scale_row
            ratios = jnp.where(inclusive, jnp.exp(jnp.where(inclusive, total - total_row, 0.0)), 0.0)
            ratios = ratios * key_scale_row
            scores_ref[head] = (reads * ratios).astype(bf16)
            lower = jnp.where(strict, rate * gram * ratios, 0.0)
            read_scale = jnp.exp(total) * query_scale
            closing = total[tokens - 1 :, :]
            write_scale = jnp.exp(closing - total) * key_scale
            parts.append((rate_row, erase_row, write_scale, jnp.exp(closing), read_scale, lower))
    return parts


def invert(parts):
    half = parts[0][5].shape[0] // 2
    inverses = unit_lower_inverses(
        [block for part in parts for block in (part[5][:half, :half], part[5][half:, half:])]
    )
    firsts, seconds = inverses[0::2], inverses[1::2]
    inner = [
        mm(part[5][half:, :half].astype(bf16), first.astype(bf16)).astype(bf16)
        for part, first in zip(parts, firsts)
    ]
    corners = [-mm(second.astype(bf16), i) for second, i in zip(seconds, inner)]
    return list(zip(firsts, seconds, corners))


def head_map(part, blocks, keys, values, map_ref, both_ref):
    rate_row, erase_row, write_scale, fade = part[:4]
    first, second, corner = blocks
    half = first.shape[0]
    key_row = lax.broadcasted_iota(jnp.int32, (DK, DK), 0)
    key_col = lax.broadcasted_iota(jnp.int32, (DK, DK), 1)

    def solved(scale_row, right):
        left_scale, right_scale = scale_row[:, :half], scale_row[:, half:]
        top = mm((first * left_scale).astype(bf16), right[:half])
        bottom = mm((corner * left_scale).astype(bf16), right[:half])
        bottom += mm((second * right_scale).astype(bf16), right[half:])
        return jnp.concatenate([top, bottom], axis=0)

    both = jnp.concatenate([solved(erase_row, keys), solved(rate_row, values)], axis=1)
    both_ref[...] = both.astype(bf16)
    summary = mm_cols(keys, (both * write_scale).astype(bf16))
    moved = jnp.where(key_row == key_col, fade, 0.0) - summary[:, :DK]
    map_ref[:, :DK] = moved.astype(bf16)
    map_ref[:, DK:] = summary[:, DK:].astype(bf16)


def layer_kernel(
    n, groups, q_hbm, k_hbm, v_hbm, gate_hbm, rate_hbm, decay_hbm, gain_hbm, weight_hbm, out_ref,
    q_ref, k_ref, v_ref, gate_ref, rate_ref, decay_ref, gain_ref, weight,
    map_ref, read_ref, own_ref, gating, scores_ref, both_ref,
    arrived, leaving, state, normed, part, out_r, out_l, in_r, in_l,
    load_sem, map_send, map_recv, state_send, state_recv,
    send_r, recv_r, send_l, recv_l,
):
    heads = map_ref.shape[0]
    apart = n // heads
    chunks, _, rows, width = part.shape
    me, spot = lax.axis_index("ctx"), lax.axis_index("tp")
    my_head = me // apart
    owner = lax.rem(me, apart) == 0

    loads = [
        pltpu.make_async_copy(source, target, load_sem.at[i])
        for i, (source, target) in enumerate((
            (k_hbm, k_ref), (q_hbm, q_ref), (rate_hbm, rate_ref), (decay_hbm, decay_ref),
            (v_hbm, v_ref), (gain_hbm, gain_ref), (gate_hbm, gate_ref), (weight_hbm, weight),
        ))
    ]
    for load in loads[:4]:
        load.start()

    barrier = pltpu.get_barrier_semaphore()
    for other in range(n):
        @pl.when(me != other)
        def _():
            pl.semaphore_signal(barrier, inc=1, device_id={"ctx": other}, device_id_type=MESH)

    after, before = lax.rem(spot + 1, groups), lax.rem(spot + groups - 1, groups)

    @pl.when(spot > 0)
    def _():
        pl.semaphore_signal(barrier, inc=1, device_id={"tp": before}, device_id_type=MESH)

    @pl.when(spot < groups - 1)
    def _():
        pl.semaphore_signal(barrier, inc=1, device_id={"tp": after}, device_id_type=MESH)

    peers = (spot > 0).astype(jnp.int32) + (spot < groups - 1).astype(jnp.int32)
    def map_copy(head, slot, target):
        return pltpu.make_async_remote_copy(
            src_ref=map_ref.at[head], dst_ref=arrived.at[slot],
            send_sem=map_send.at[head], recv_sem=map_recv.at[slot],
            device_id={"ctx": target}, device_id_type=MESH,
        )

    key_heads = k_ref.shape[1] // DK
    sharing = heads // key_heads
    for load in loads[:4]:
        load.wait()
    for load in loads[4:]:
        load.start()
    parts = prepare(key_heads, sharing, q_ref, k_ref, rate_ref, decay_ref, scores_ref)
    blocks = invert(parts)
    loads[4].wait()
    for head in range(heads):
        place = slice(head * DV, (head + 1) * DV)
        group = head // sharing
        keys = k_ref[:, group * DK : (group + 1) * DK]
        head_map(
            parts[head], blocks[head], keys, v_ref[:, place], map_ref.at[head], both_ref.at[head]
        )
        if head == 0:
            pl.semaphore_wait(barrier, n - 1 + peers)

        @pl.when((me != head * apart) & (me < n - 1))
        def _():
            map_copy(head, me, head * apart).start()

    for head in range(heads):
        place = slice(head * DV, (head + 1) * DV)
        group = head // sharing
        queries = q_ref[:, group * DK : (group + 1) * DK].astype(f32)
        seen = mm(scores_ref[head], both_ref[head])
        read_ref[:, place] = (parts[head][4] * queries - seen[:, :DK]).astype(bf16)
        own_ref[:, place] = seen[:, DK:]

    for load in loads[5:]:
        load.wait()
    gain = gain_ref[...]
    for head in range(heads):
        place = slice(head * DV, (head + 1) * DV)
        gate = gate_ref[:, place].astype(f32)
        gating[:, place] = gain * (gate / (1.0 + jnp.exp(-gate)))

    def state_copy(head, target):
        return pltpu.make_async_remote_copy(
            src_ref=leaving.at[target], dst_ref=state.at[head],
            send_sem=state_send.at[target], recv_sem=state_recv.at[head],
            device_id={"ctx": target}, device_id_type=MESH,
        )

    @pl.when(me == 0)
    def _():
        state[...] = jnp.zeros_like(state)

    @pl.when(owner)
    def _():
        arrived[pl.ds(me, 1)] = map_ref[pl.ds(my_head, 1)]
        current = jnp.zeros((DK, DV), f32)
        for step in range(n - 1):
            @pl.when(me != step)
            def _():
                map_copy(0, step, step).wait_recv()

            high = current.astype(bf16)
            low = (current - high.astype(f32)).astype(bf16)
            turned = mm(arrived[step, :, :DK], jnp.concatenate([high, low], axis=1))
            current = turned[:, :DV] + turned[:, DV:] + arrived[step, :, DK:].astype(f32)

            @pl.when(me != step + 1)
            def _():
                leaving[step + 1] = current.astype(bf16)
                state_copy(my_head, step + 1).start()

            @pl.when(me == step + 1)
            def _():
                state[pl.ds(my_head, 1)] = current.astype(bf16)[None]

    for head in range(heads):
        @pl.when((me > 0) & (me != head * apart))
        def _():
            state_copy(head, 0).wait_recv()

        place = slice(head * DV, (head + 1) * DV)
        core = mm(read_ref[:, place], state[head]) + own_ref[:, place]
        square_mean = jnp.mean(core * core, axis=1, keepdims=True)
        normed[:, place] = (core * lax.rsqrt(square_mean + 1e-06) * gating[:, place]).astype(bf16)

    def right_copy(source, c, target):
        return pltpu.make_async_remote_copy(
            src_ref=source.at[c, target], dst_ref=in_r.at[c, target],
            send_sem=send_r.at[c, target], recv_sem=recv_r.at[c, target],
            device_id={"tp": after}, device_id_type=MESH,
        )

    def left_copy(source, c, target):
        return pltpu.make_async_remote_copy(
            src_ref=source.at[c, target], dst_ref=in_l.at[c, target],
            send_sem=send_l.at[c, target], recv_sem=recv_l.at[c, target],
            device_id={"tp": before}, device_id_type=MESH,
        )

    @pl.when(spot == 0)
    def _():
        in_r[:, 0] = jnp.zeros_like(in_r[:, 0])

    @pl.when(spot == groups - 1)
    def _():
        in_l[:, groups - 1] = jnp.zeros_like(in_l[:, groups - 1])

    to_right = [(c, target) for c in range(chunks) for target in range(groups - 1, 0, -1)]
    to_left = [(c, target) for c in range(chunks) for target in range(groups - 1)]
    window = 2

    def feed(copy, order, c):
        for i, unit in enumerate(order):
            if unit[0] == c:
                if i >= window:
                    copy(part, *order[i - window]).wait_send()
                copy(part, *unit).start()

    for c in range(chunks):
        product = mm(normed[...], weight[:, c * width : (c + 1) * width]).astype(bf16)
        part[c] = product.reshape(groups, rows, width)

        @pl.when(spot == 0)
        def _():
            feed(right_copy, to_right, c)

        @pl.when(spot == groups - 1)
        def _():
            feed(left_copy, to_left, c)

    for c in range(chunks):
        def relay(step, carry):
            far = groups - 1 - step

            @pl.when((spot > 0) & (far > spot))
            def _():
                right_copy(part, c, far).wait_recv()
                out_r[c, far] = (in_r[c, far].astype(f32) + part[c, far].astype(f32)).astype(bf16)
                right_copy(out_r, c, far).start()

            @pl.when((spot < groups - 1) & (step < spot))
            def _():
                left_copy(part, c, step).wait_recv()
                out_l[c, step] = (in_l[c, step].astype(f32) + part[c, step].astype(f32)).astype(bf16)
                left_copy(out_l, c, step).start()

            return carry

        lax.fori_loop(0, groups - 1, relay, 0)

    for c in range(chunks):
        @pl.when(spot > 0)
        def _():
            right_copy(part, c, spot).wait_recv()

        @pl.when(spot < groups - 1)
        def _():
            left_copy(part, c, spot).wait_recv()

        mixed = part[c, spot].astype(f32) + in_r[c, spot].astype(f32) + in_l[c, spot].astype(f32)
        out_ref[:, c * width : (c + 1) * width] = mixed.astype(bf16)

    for head in range(heads):
        @pl.when((me != head * apart) & (me < n - 1))
        def _():
            map_copy(head, me, head * apart).wait_send()

    for target in range(1, n):
        @pl.when(owner & (me != target))
        def _():
            state_copy(my_head, target).wait_send()

    for c in range(chunks):
        def drain(target, carry):
            @pl.when((target > spot) & (spot > 0))
            def _():
                right_copy(part, c, target).wait_send()

            @pl.when((target < spot) & (spot < groups - 1))
            def _():
                left_copy(part, c, target).wait_send()

            return carry

        lax.fori_loop(0, groups, drain, 0)

    @pl.when(spot == 0)
    def _():
        for unit in to_right[-window:]:
            right_copy(part, *unit).wait_send()

    @pl.when(spot == groups - 1)
    def _():
        for unit in to_left[-window:]:
            left_copy(part, *unit).wait_send()


def local(n, groups, queries, key_vectors, value_vectors, output_gate, write_rate, log_decay, norm_gain, out_weight):
    tokens = queries.shape[0]
    heads = value_vectors.shape[1] // DV
    features, model = out_weight.shape
    rows = tokens // groups
    chunks = 4
    width = model // chunks
    piece = pltpu.VMEM((chunks, groups, rows, width), bf16)
    dma = pltpu.SemaphoreType.DMA
    inputs = (
        queries, key_vectors, value_vectors, output_gate,
        write_rate.T, log_decay.T, norm_gain.reshape(1, DV), out_weight,
    )
    return pl.pallas_call(
        functools.partial(layer_kernel, n, groups),
        in_specs=[pl.BlockSpec(memory_space=pl.ANY)] * len(inputs),
        out_specs=pl.BlockSpec(memory_space=pltpu.VMEM),
        out_shape=jax.ShapeDtypeStruct((rows, model), bf16),
        scratch_shapes=[pltpu.VMEM(array.shape, array.dtype) for array in inputs] + [
            pltpu.VMEM((heads, DK, DK + DV), bf16),
            pltpu.VMEM((tokens, features), bf16),
            pltpu.VMEM((tokens, features), f32),
            pltpu.VMEM((tokens, features), f32),
            pltpu.VMEM((heads, tokens, tokens), bf16),
            pltpu.VMEM((heads, tokens, DK + DV), bf16),
            pltpu.VMEM((n, DK, DK + DV), bf16),
            pltpu.VMEM((n, DK, DV), bf16),
            pltpu.VMEM((heads, DK, DV), bf16),
            pltpu.VMEM((tokens, features), bf16),
            piece, piece, piece, piece, piece,
            dma((len(inputs),)), dma((heads,)), dma((n,)), dma((n,)), dma((heads,)),
            dma((chunks, groups)), dma((chunks, groups)), dma((chunks, groups)), dma((chunks, groups)),
        ],
        compiler_params=pltpu.CompilerParams(
            collective_id=0, has_side_effects=True, vmem_limit_bytes=40 * 2**20
        ),
    )(*inputs)


def solution(mesh):
    placed = (
        P("ctx", "tp"),
        P("ctx", "tp"),
        P("ctx", "tp"),
        P("ctx", "tp"),
        P("ctx", "tp"),
        P("ctx", "tp"),
        P(),
        P("tp", None),
    )
    body = functools.partial(local, mesh.shape["ctx"], mesh.shape["tp"])
    return jax.shard_map(
        body, mesh=mesh, in_specs=placed, out_specs=P(("ctx", "tp"), None), check_vma=False
    )
```

```python
import functools

import jax
import jax.numpy as jnp
from jax import lax
from jax.experimental import pallas as pl
from jax.experimental.pallas import tpu as pltpu
from jax.sharding import PartitionSpec as P

DK = 128
DV = 128
MESH = pl.DeviceIdType.MESH
f32, bf16 = jnp.float32, jnp.bfloat16


def mm(left, right):
    return jnp.dot(left, right, preferred_element_type=f32)


def mm_rows(left, right):
    return lax.dot_general(left, right, (((1,), (1,)), ((), ())), preferred_element_type=f32)


def mm_cols(left, right):
    return lax.dot_general(left, right, (((0,), (0,)), ((), ())), preferred_element_type=f32)


def unit_lower_inverses(lowers):
    size = lowers[0].shape[0]
    row = lax.broadcasted_iota(jnp.int32, (size, size), 0)
    col = lax.broadcasted_iota(jnp.int32, (size, size), 1)
    apart = row ^ col
    eye = jnp.where(row == col, 1.0, 0.0)
    inverses = [eye - jnp.where(apart == 1, lower, 0.0) for lower in lowers]
    step = 2
    while step < size:
        coupling = (apart >= step) & (apart < 2 * step)
        rounded = [inverse.astype(bf16) for inverse in inverses]
        inner = [
            mm(jnp.where(coupling, lower, 0.0).astype(bf16), r).astype(bf16)
            for lower, r in zip(lowers, rounded)
        ]
        inverses = [inverse - mm(r, i) for inverse, r, i in zip(inverses, rounded, inner)]
        step *= 2
    rounded = [inverse.astype(bf16) for inverse in inverses]
    highs = [lower.astype(bf16) for lower in lowers]
    lows = [(lower - high.astype(f32)).astype(bf16) for lower, high in zip(lowers, highs)]
    residuals = [
        (eye - r.astype(f32) - mm(high, r) - mm(low, r)).astype(bf16)
        for high, low, r in zip(highs, lows, rounded)
    ]
    return [r.astype(f32) + mm(r, residual) for r, residual in zip(rounded, residuals)]


def square_sums(source, key_heads, sharing):
    lane = lax.broadcasted_iota(jnp.int32, (DK, 128), 1)
    sums = 0.0
    for group in range(key_heads):
        mine = (lane >= group * sharing) & (lane < (group + 1) * sharing)
        chosen = jnp.where(mine, 1.0, 0.0).astype(bf16)
        values = source[:, group * DK : (group + 1) * DK].astype(f32)
        squares = values * values
        high = squares.astype(bf16)
        sums = sums + mm(high, chosen) + mm((squares - high.astype(f32)).astype(bf16), chosen)
    return sums


def prepare(key_heads, sharing, q_ref, k_ref, rate_ref, decay_ref, turn_ref, scores_ref):
    tokens, heads = q_ref.shape[0], rate_ref.shape[0]
    half = tokens // 2
    row = lax.broadcasted_iota(jnp.int32, (tokens, tokens), 0)
    col = lax.broadcasted_iota(jnp.int32, (tokens, tokens), 1)
    upper = jnp.where(row <= col, 1.0, 0.0)
    total_rows = jnp.dot(
        decay_ref[...], upper, precision=lax.Precision.HIGHEST, preferred_element_type=f32
    )
    rate_rows = rate_ref[...]
    turn_ref[...] = jnp.zeros_like(turn_ref)
    turn_ref[0, :heads] = rate_rows
    turn_ref[1, :heads] = total_rows
    rate, total = turn_ref[0].T, turn_ref[1].T
    key_scale = lax.rsqrt(square_sums(k_ref, key_heads, sharing) + 1e-06)
    query_scale = lax.rsqrt(square_sums(q_ref, key_heads, sharing) + 1e-06)
    key_rows = key_scale.T[:heads]
    erase_rows = rate_rows * jnp.exp(total_rows) * key_rows
    closing = total[tokens - 1 :, :]
    fade = jnp.exp(closing)
    write_scale = jnp.exp(closing - total) * key_scale
    strength = rate * key_scale

    half_row = lax.broadcasted_iota(jnp.int32, (half, half), 0)
    half_col = lax.broadcasted_iota(jnp.int32, (half, half), 1)
    inclusive, strict = half_row >= half_col, half_row > half_col
    parts = []
    for group in range(key_heads):
        key_place = slice(group * DK, (group + 1) * DK)
        queries, keys = q_ref[:, key_place], k_ref[:, key_place]
        gram = mm_rows(keys, keys)
        reads = mm_rows(queries, keys)
        for head in range(group * sharing, (group + 1) * sharing):
            here = slice(head, head + 1)
            total_row, key_row = total_rows[here], key_rows[here]

            def spread(rows, cols):
                return jnp.exp(total[rows, here] - total_row[:, cols])

            top, low = slice(0, half), slice(half, tokens)
            ratio_a = jnp.where(inclusive, spread(top, top), 0.0) * key_row[:, top]
            ratio_b = jnp.where(inclusive, spread(low, low), 0.0) * key_row[:, low]
            ratio_c = spread(low, top) * key_row[:, top]
            scores_ref[head, :half, :half] = (reads[top, top] * ratio_a).astype(bf16)
            scores_ref[head, half:, :half] = (reads[low, top] * ratio_c).astype(bf16)
            scores_ref[head, half:, half:] = (reads[low, low] * ratio_b).astype(bf16)
            lower_a = jnp.where(strict, gram[top, top] * ratio_a * strength[top, here], 0.0)
            lower_b = jnp.where(strict, gram[low, low] * ratio_b * strength[low, here], 0.0)
            lower_c = (gram[low, top] * ratio_c * strength[low, here]).astype(bf16)
            parts.append((
                rate_rows[here], erase_rows[here], write_scale[:, here], fade[:, here],
                jnp.exp(total[:, here]), query_scale[:, here], lower_a, lower_b, lower_c,
            ))
    return parts


def invert(parts):
    inverses = unit_lower_inverses([block for part in parts for block in part[6:8]])
    firsts, seconds = inverses[0::2], inverses[1::2]
    inner = [mm(part[8], first.astype(bf16)).astype(bf16) for part, first in zip(parts, firsts)]
    corners = [-mm(second.astype(bf16), i) for second, i in zip(seconds, inner)]
    return list(zip(firsts, seconds, corners))


def head_map(part, blocks, keys, values, map_ref, both_ref):
    rate_row, erase_row, write_scale, fade = part[:4]
    first, second, corner = blocks
    half = first.shape[0]
    key_row = lax.broadcasted_iota(jnp.int32, (DK, DK), 0)
    key_col = lax.broadcasted_iota(jnp.int32, (DK, DK), 1)

    def solved(scale_row, right):
        left_scale, right_scale = scale_row[:, :half], scale_row[:, half:]
        top = mm((first * left_scale).astype(bf16), right[:half])
        bottom = mm((corner * left_scale).astype(bf16), right[:half])
        bottom += mm((second * right_scale).astype(bf16), right[half:])
        return jnp.concatenate([top, bottom], axis=0)

    both = jnp.concatenate([solved(erase_row, keys), solved(rate_row, values)], axis=1)
    both_ref[...] = both.astype(bf16)
    summary = mm_cols(keys, (both * write_scale).astype(bf16))
    moved = jnp.where(key_row == key_col, fade, 0.0) - summary[:, :DK]
    map_ref[:, :DK] = moved.astype(bf16)
    map_ref[:, DK:] = summary[:, DK:].astype(bf16)


def layer_kernel(
    n, groups, q_hbm, k_hbm, v_hbm, gate_hbm, rate_hbm, decay_hbm, gain_hbm, weight_hbm, out_ref,
    q_ref, k_ref, v_ref, gate_ref, rate_ref, decay_ref, gain_ref, weight,
    map_ref, read_ref, own_ref, gating, turn_ref, scores_ref, both_ref,
    arrived, leaving, state, normed, part, out_r, out_l, in_r, in_l,
    load_sem, map_send, map_recv, state_send, state_recv,
    send_r, recv_r, send_l, recv_l,
):
    heads = map_ref.shape[0]
    apart = n // heads
    chunks, _, rows, width = part.shape
    me, spot = lax.axis_index("ctx"), lax.axis_index("tp")
    my_head = me // apart
    owner = lax.rem(me, apart) == 0

    loads = [
        pltpu.make_async_copy(source, target, load_sem.at[i])
        for i, (source, target) in enumerate((
            (k_hbm, k_ref), (q_hbm, q_ref), (rate_hbm, rate_ref), (decay_hbm, decay_ref),
            (v_hbm, v_ref), (gain_hbm, gain_ref), (gate_hbm, gate_ref), (weight_hbm, weight),
        ))
    ]
    for load in loads[:4]:
        load.start()

    barrier = pltpu.get_barrier_semaphore()
    for other in range(n):
        @pl.when(me != other)
        def _():
            pl.semaphore_signal(barrier, inc=1, device_id={"ctx": other}, device_id_type=MESH)

    after, before = lax.rem(spot + 1, groups), lax.rem(spot + groups - 1, groups)

    @pl.when(spot > 0)
    def _():
        pl.semaphore_signal(barrier, inc=1, device_id={"tp": before}, device_id_type=MESH)

    @pl.when(spot < groups - 1)
    def _():
        pl.semaphore_signal(barrier, inc=1, device_id={"tp": after}, device_id_type=MESH)

    peers = (spot > 0).astype(jnp.int32) + (spot < groups - 1).astype(jnp.int32)
    def map_copy(head, slot, target):
        return pltpu.make_async_remote_copy(
            src_ref=map_ref.at[head], dst_ref=arrived.at[slot],
            send_sem=map_send.at[head], recv_sem=map_recv.at[slot],
            device_id={"ctx": target}, device_id_type=MESH,
        )

    key_heads = k_ref.shape[1] // DK
    sharing = heads // key_heads
    for load in loads[:4]:
        load.wait()
    for load in loads[4:]:
        load.start()
    parts = prepare(key_heads, sharing, q_ref, k_ref, rate_ref, decay_ref, turn_ref, scores_ref)
    blocks = invert(parts)
    loads[4].wait()
    for head in range(heads):
        place = slice(head * DV, (head + 1) * DV)
        group = head // sharing
        keys = k_ref[:, group * DK : (group + 1) * DK]
        head_map(
            parts[head], blocks[head], keys, v_ref[:, place], map_ref.at[head], both_ref.at[head]
        )
        if head == 0:
            pl.semaphore_wait(barrier, n - 1 + peers)

        @pl.when((me != head * apart) & (me < n - 1))
        def _():
            map_copy(head, me, head * apart).start()

    half = q_ref.shape[0] // 2
    for head in range(heads):
        place = slice(head * DV, (head + 1) * DV)
        group = head // sharing
        queries = q_ref[:, group * DK : (group + 1) * DK].astype(f32)
        decayed, query_scale = parts[head][4:6]
        top = mm(scores_ref[head, :half, :half], both_ref[head, :half])
        low = mm(scores_ref[head, half:], both_ref[head])
        seen = jnp.concatenate([top, low], axis=0)
        read_ref[:, place] = ((decayed * queries - seen[:, :DK]) * query_scale).astype(bf16)
        own_ref[:, place] = seen[:, DK:] * query_scale

    for load in loads[5:]:
        load.wait()
    gain = gain_ref[...]
    for head in range(heads):
        place = slice(head * DV, (head + 1) * DV)
        gate = gate_ref[:, place].astype(f32)
        gating[:, place] = gain * (gate / (1.0 + jnp.exp(-gate)))

    def state_copy(head, target):
        return pltpu.make_async_remote_copy(
            src_ref=leaving.at[target], dst_ref=state.at[head],
            send_sem=state_send.at[target], recv_sem=state_recv.at[head],
            device_id={"ctx": target}, device_id_type=MESH,
        )

    @pl.when(me == 0)
    def _():
        state[...] = jnp.zeros_like(state)

    @pl.when(owner)
    def _():
        arrived[pl.ds(me, 1)] = map_ref[pl.ds(my_head, 1)]
        for step in range(n - 1):
            @pl.when(me != step)
            def _():
                map_copy(0, step, step).wait_recv()

        current = arrived[0, :, DK:].astype(f32)
        for step in range(n - 1):
            if step > 0:
                high = current.astype(bf16)
                low = (current - high.astype(f32)).astype(bf16)
                turned = mm(arrived[step, :, :DK], jnp.concatenate([high, low], axis=1))
                current = turned[:, :DV] + turned[:, DV:] + arrived[step, :, DK:].astype(f32)
            leaving[step + 1] = current.astype(bf16)

            @pl.when(me != step + 1)
            def _():
                state_copy(my_head, step + 1).start()

        @pl.when(me > 0)
        def _():
            state[pl.ds(my_head, 1)] = leaving[pl.ds(me, 1)]

    for head in range(heads):
        @pl.when((me > 0) & (me != head * apart))
        def _():
            state_copy(head, 0).wait_recv()

    ones = jnp.ones((DV, DV), bf16)
    for head in range(heads):
        place = slice(head * DV, (head + 1) * DV)
        core = mm(read_ref[:, place], state[head]) + own_ref[:, place]
        square_mean = mm((core * core).astype(bf16), ones) * (1.0 / DV)
        normed[:, place] = (core * lax.rsqrt(square_mean + 1e-06) * gating[:, place]).astype(bf16)

    def right_copy(source, c, target):
        return pltpu.make_async_remote_copy(
            src_ref=source.at[c, target], dst_ref=in_r.at[c, target],
            send_sem=send_r.at[c, target], recv_sem=recv_r.at[c, target],
            device_id={"tp": after}, device_id_type=MESH,
        )

    def left_copy(source, c, target):
        return pltpu.make_async_remote_copy(
            src_ref=source.at[c, target], dst_ref=in_l.at[c, target],
            send_sem=send_l.at[c, target], recv_sem=recv_l.at[c, target],
            device_id={"tp": before}, device_id_type=MESH,
        )

    @pl.when(spot == 0)
    def _():
        in_r[:, 0] = jnp.zeros_like(in_r[:, 0])

    @pl.when(spot == groups - 1)
    def _():
        in_l[:, groups - 1] = jnp.zeros_like(in_l[:, groups - 1])

    to_right = [(c, target) for c in range(chunks) for target in range(groups - 1, 0, -1)]
    to_left = [(c, target) for c in range(chunks) for target in range(groups - 1)]
    window = 2

    def feed(copy, order, c):
        for i, unit in enumerate(order):
            if unit[0] == c:
                if i >= window:
                    copy(part, *order[i - window]).wait_send()
                copy(part, *unit).start()

    for c in range(chunks):
        product = mm(normed[...], weight[:, c * width : (c + 1) * width]).astype(bf16)
        part[c] = product.reshape(groups, rows, width)

        @pl.when(spot == 0)
        def _():
            feed(right_copy, to_right, c)

        @pl.when(spot == groups - 1)
        def _():
            feed(left_copy, to_left, c)

    for c in range(chunks):
        def relay(step, carry):
            far = groups - 1 - step

            @pl.when((spot > 0) & (far > spot))
            def _():
                right_copy(part, c, far).wait_recv()
                out_r[c, far] = (in_r[c, far].astype(f32) + part[c, far].astype(f32)).astype(bf16)
                right_copy(out_r, c, far).start()

            @pl.when((spot < groups - 1) & (step < spot))
            def _():
                left_copy(part, c, step).wait_recv()
                out_l[c, step] = (in_l[c, step].astype(f32) + part[c, step].astype(f32)).astype(bf16)
                left_copy(out_l, c, step).start()

            return carry

        lax.fori_loop(0, groups - 1, relay, 0)

    for c in range(chunks):
        @pl.when(spot > 0)
        def _():
            right_copy(part, c, spot).wait_recv()

        @pl.when(spot < groups - 1)
        def _():
            left_copy(part, c, spot).wait_recv()

        mixed = part[c, spot].astype(f32) + in_r[c, spot].astype(f32) + in_l[c, spot].astype(f32)
        out_ref[:, c * width : (c + 1) * width] = mixed.astype(bf16)

    for head in range(heads):
        @pl.when((me != head * apart) & (me < n - 1))
        def _():
            map_copy(head, me, head * apart).wait_send()

    for target in range(1, n):
        @pl.when(owner & (me != target))
        def _():
            state_copy(my_head, target).wait_send()

    for c in range(chunks):
        def drain(target, carry):
            @pl.when((target > spot) & (spot > 0))
            def _():
                right_copy(part, c, target).wait_send()

            @pl.when((target < spot) & (spot < groups - 1))
            def _():
                left_copy(part, c, target).wait_send()

            return carry

        lax.fori_loop(0, groups, drain, 0)

    @pl.when(spot == 0)
    def _():
        for unit in to_right[-window:]:
            right_copy(part, *unit).wait_send()

    @pl.when(spot == groups - 1)
    def _():
        for unit in to_left[-window:]:
            left_copy(part, *unit).wait_send()


def local(n, groups, queries, key_vectors, value_vectors, output_gate, write_rate, log_decay, norm_gain, out_weight):
    tokens = queries.shape[0]
    heads = value_vectors.shape[1] // DV
    features, model = out_weight.shape
    rows = tokens // groups
    chunks = 4
    width = model // chunks
    piece = pltpu.VMEM((chunks, groups, rows, width), bf16)
    dma = pltpu.SemaphoreType.DMA
    inputs = (
        queries, key_vectors, value_vectors, output_gate,
        write_rate.T, log_decay.T, norm_gain.reshape(1, DV), out_weight,
    )
    return pl.pallas_call(
        functools.partial(layer_kernel, n, groups),
        in_specs=[pl.BlockSpec(memory_space=pl.ANY)] * len(inputs),
        out_specs=pl.BlockSpec(memory_space=pltpu.VMEM),
        out_shape=jax.ShapeDtypeStruct((rows, model), bf16),
        scratch_shapes=[pltpu.VMEM(array.shape, array.dtype) for array in inputs] + [
            pltpu.VMEM((heads, DK, DK + DV), bf16),
            pltpu.VMEM((tokens, features), bf16),
            pltpu.VMEM((tokens, features), f32),
            pltpu.VMEM((tokens, features), f32),
            pltpu.VMEM((2, 128, tokens), f32),
            pltpu.VMEM((heads, tokens, tokens), bf16),
            pltpu.VMEM((heads, tokens, DK + DV), bf16),
            pltpu.VMEM((n, DK, DK + DV), bf16),
            pltpu.VMEM((n, DK, DV), bf16),
            pltpu.VMEM((heads, DK, DV), bf16),
            pltpu.VMEM((tokens, features), bf16),
            piece, piece, piece, piece, piece,
            dma((len(inputs),)), dma((heads,)), dma((n,)), dma((n,)), dma((heads,)),
            dma((chunks, groups)), dma((chunks, groups)), dma((chunks, groups)), dma((chunks, groups)),
        ],
        compiler_params=pltpu.CompilerParams(
            collective_id=0, has_side_effects=True, vmem_limit_bytes=56 * 2**20
        ),
    )(*inputs)


def solution(mesh):
    placed = (
        P("ctx", "tp"),
        P("ctx", "tp"),
        P("ctx", "tp"),
        P("ctx", "tp"),
        P("ctx", "tp"),
        P("ctx", "tp"),
        P(),
        P("tp", None),
    )
    body = functools.partial(local, mesh.shape["ctx"], mesh.shape["tp"])
    return jax.shard_map(
        body, mesh=mesh, in_specs=placed, out_specs=P(("ctx", "tp"), None), check_vma=False
    )
```

```python
import functools

import jax
import jax.numpy as jnp
from jax import lax
from jax.experimental import pallas as pl
from jax.experimental.pallas import tpu as pltpu
from jax.sharding import PartitionSpec as P

DK = 128
DV = 128
MESH = pl.DeviceIdType.MESH
f32, bf16 = jnp.float32, jnp.bfloat16


def mm(left, right):
    return jnp.dot(left, right, preferred_element_type=f32)


def mm_rows(left, right):
    return lax.dot_general(left, right, (((1,), (1,)), ((), ())), preferred_element_type=f32)


def mm_cols(left, right):
    return lax.dot_general(left, right, (((0,), (0,)), ((), ())), preferred_element_type=f32)


def unit_lower_inverses(lowers):
    size = lowers[0].shape[0]
    row = lax.broadcasted_iota(jnp.int32, (size, size), 0)
    col = lax.broadcasted_iota(jnp.int32, (size, size), 1)
    apart = row ^ col
    eye = jnp.where(row == col, 1.0, 0.0)
    inverses = [eye - jnp.where(apart == 1, lower, 0.0) for lower in lowers]
    step = 2
    while step < size:
        coupling = (apart >= step) & (apart < 2 * step)
        rounded = [inverse.astype(bf16) for inverse in inverses]
        inner = [
            mm(jnp.where(coupling, lower, 0.0).astype(bf16), r).astype(bf16)
            for lower, r in zip(lowers, rounded)
        ]
        inverses = [inverse - mm(r, i) for inverse, r, i in zip(inverses, rounded, inner)]
        step *= 2
    rounded = [inverse.astype(bf16) for inverse in inverses]
    highs = [lower.astype(bf16) for lower in lowers]
    lows = [(lower - high.astype(f32)).astype(bf16) for lower, high in zip(lowers, highs)]
    residuals = [
        (eye - r.astype(f32) - mm(high, r) - mm(low, r)).astype(bf16)
        for high, low, r in zip(highs, lows, rounded)
    ]
    return [r.astype(f32) + mm(r, residual) for r, residual in zip(rounded, residuals)]


def square_sums(source, key_heads, sharing):
    lane = lax.broadcasted_iota(jnp.int32, (DK, 128), 1)
    sums = 0.0
    for group in range(key_heads):
        mine = (lane >= group * sharing) & (lane < (group + 1) * sharing)
        chosen = jnp.where(mine, 1.0, 0.0).astype(bf16)
        values = source[:, group * DK : (group + 1) * DK].astype(f32)
        squares = values * values
        high = squares.astype(bf16)
        sums = sums + mm(high, chosen) + mm((squares - high.astype(f32)).astype(bf16), chosen)
    return sums


def prepare(key_heads, sharing, q_ref, k_ref, rate_ref, decay_ref, turn_ref, scores_ref):
    tokens, heads = q_ref.shape[0], rate_ref.shape[0]
    half = tokens // 2
    row = lax.broadcasted_iota(jnp.int32, (tokens, tokens), 0)
    col = lax.broadcasted_iota(jnp.int32, (tokens, tokens), 1)
    upper = jnp.where(row <= col, 1.0, 0.0)
    total_rows = jnp.dot(
        decay_ref[...], upper, precision=lax.Precision.HIGHEST, preferred_element_type=f32
    )
    rate_rows = rate_ref[...]
    turn_ref[...] = jnp.zeros_like(turn_ref)
    turn_ref[0, :heads] = rate_rows
    turn_ref[1, :heads] = total_rows
    rate, total = turn_ref[0].T, turn_ref[1].T
    key_scale = lax.rsqrt(square_sums(k_ref, key_heads, sharing) + 1e-06)
    query_scale = lax.rsqrt(square_sums(q_ref, key_heads, sharing) + 1e-06)
    key_rows = key_scale.T[:heads]
    erase_rows = rate_rows * jnp.exp(total_rows) * key_rows
    closing = total[tokens - 1 :, :]
    fade = jnp.exp(closing)
    write_scale = jnp.exp(closing - total) * key_scale
    strength = rate * key_scale

    half_row = lax.broadcasted_iota(jnp.int32, (half, half), 0)
    half_col = lax.broadcasted_iota(jnp.int32, (half, half), 1)
    inclusive, strict = half_row >= half_col, half_row > half_col
    parts = []
    for group in range(key_heads):
        key_place = slice(group * DK, (group + 1) * DK)
        queries, keys = q_ref[:, key_place], k_ref[:, key_place]
        gram = mm_rows(keys, keys)
        reads = mm_rows(queries, keys)
        for head in range(group * sharing, (group + 1) * sharing):
            here = slice(head, head + 1)
            total_row, key_row = total_rows[here], key_rows[here]

            def spread(rows, cols):
                return jnp.exp(total[rows, here] - total_row[:, cols])

            top, low = slice(0, half), slice(half, tokens)
            ratio_a = jnp.where(inclusive, spread(top, top), 0.0) * key_row[:, top]
            ratio_b = jnp.where(inclusive, spread(low, low), 0.0) * key_row[:, low]
            ratio_c = spread(low, top) * key_row[:, top]
            scores_ref[head, :half, :half] = (reads[top, top] * ratio_a).astype(bf16)
            scores_ref[head, half:, :half] = (reads[low, top] * ratio_c).astype(bf16)
            scores_ref[head, half:, half:] = (reads[low, low] * ratio_b).astype(bf16)
            lower_a = jnp.where(strict, gram[top, top] * ratio_a * strength[top, here], 0.0)
            lower_b = jnp.where(strict, gram[low, low] * ratio_b * strength[low, here], 0.0)
            lower_c = (gram[low, top] * ratio_c * strength[low, here]).astype(bf16)
            parts.append((
                rate_rows[here], erase_rows[here], write_scale[:, here], fade[:, here],
                jnp.exp(total[:, here]), query_scale[:, here], lower_a, lower_b, lower_c,
            ))
    return parts


def invert(parts):
    inverses = unit_lower_inverses([block for part in parts for block in part[6:8]])
    firsts, seconds = inverses[0::2], inverses[1::2]
    inner = [mm(part[8], first.astype(bf16)).astype(bf16) for part, first in zip(parts, firsts)]
    corners = [-mm(second.astype(bf16), i) for second, i in zip(seconds, inner)]
    return list(zip(firsts, seconds, corners))


def head_map(part, blocks, keys, values, map_ref, both_ref):
    rate_row, erase_row, write_scale, fade = part[:4]
    first, second, corner = blocks
    half = first.shape[0]
    key_row = lax.broadcasted_iota(jnp.int32, (DK, DK), 0)
    key_col = lax.broadcasted_iota(jnp.int32, (DK, DK), 1)

    def solved(scale_row, right):
        left_scale, right_scale = scale_row[:, :half], scale_row[:, half:]
        top = mm((first * left_scale).astype(bf16), right[:half])
        bottom = mm((corner * left_scale).astype(bf16), right[:half])
        bottom += mm((second * right_scale).astype(bf16), right[half:])
        return jnp.concatenate([top, bottom], axis=0)

    both = jnp.concatenate([solved(erase_row, keys), solved(rate_row, values)], axis=1)
    both_ref[...] = both.astype(bf16)
    summary = mm_cols(keys, (both * write_scale).astype(bf16))
    moved = jnp.where(key_row == key_col, fade, 0.0) - summary[:, :DK]
    map_ref[:, :DK] = moved.astype(bf16)
    map_ref[:, DK:] = summary[:, DK:].astype(bf16)


def layer_kernel(
    n, q_hbm, k_hbm, v_hbm, gate_hbm, rate_hbm, decay_hbm, gain_hbm, normed,
    q_ref, k_ref, v_ref, gate_ref, rate_ref, decay_ref, gain_ref,
    map_ref, read_ref, own_ref, gating, turn_ref, scores_ref, both_ref,
    arrived, leaving, state,
    load_sem, map_send, map_recv, state_send, state_recv,
):
    heads = map_ref.shape[0]
    apart = n // heads
    me = lax.axis_index("ctx")
    my_head = me // apart
    owner = lax.rem(me, apart) == 0

    loads = [
        pltpu.make_async_copy(source, target, load_sem.at[i])
        for i, (source, target) in enumerate((
            (k_hbm, k_ref), (q_hbm, q_ref), (rate_hbm, rate_ref), (decay_hbm, decay_ref),
            (v_hbm, v_ref), (gain_hbm, gain_ref), (gate_hbm, gate_ref),
        ))
    ]
    for load in loads[:4]:
        load.start()

    barrier = pltpu.get_barrier_semaphore()
    for other in range(n):
        @pl.when(me != other)
        def _():
            pl.semaphore_signal(barrier, inc=1, device_id={"ctx": other}, device_id_type=MESH)

    def map_copy(head, slot, target):
        return pltpu.make_async_remote_copy(
            src_ref=map_ref.at[head], dst_ref=arrived.at[slot],
            send_sem=map_send.at[head], recv_sem=map_recv.at[slot],
            device_id={"ctx": target}, device_id_type=MESH,
        )

    key_heads = k_ref.shape[1] // DK
    sharing = heads // key_heads
    for load in loads[:4]:
        load.wait()
    for load in loads[4:]:
        load.start()
    parts = prepare(key_heads, sharing, q_ref, k_ref, rate_ref, decay_ref, turn_ref, scores_ref)
    blocks = invert(parts)
    loads[4].wait()
    for head in range(heads):
        place = slice(head * DV, (head + 1) * DV)
        group = head // sharing
        keys = k_ref[:, group * DK : (group + 1) * DK]
        head_map(
            parts[head], blocks[head], keys, v_ref[:, place], map_ref.at[head], both_ref.at[head]
        )
        if head == 0:
            pl.semaphore_wait(barrier, n - 1)

        @pl.when((me != head * apart) & (me < n - 1))
        def _():
            map_copy(head, me, head * apart).start()

    half = q_ref.shape[0] // 2
    for head in range(heads):
        place = slice(head * DV, (head + 1) * DV)
        group = head // sharing
        queries = q_ref[:, group * DK : (group + 1) * DK].astype(f32)
        decayed, query_scale = parts[head][4:6]
        top = mm(scores_ref[head, :half, :half], both_ref[head, :half])
        low = mm(scores_ref[head, half:], both_ref[head])
        seen = jnp.concatenate([top, low], axis=0)
        read_ref[:, place] = ((decayed * queries - seen[:, :DK]) * query_scale).astype(bf16)
        own_ref[:, place] = seen[:, DK:] * query_scale

    for load in loads[5:]:
        load.wait()
    gain = gain_ref[...]
    for head in range(heads):
        place = slice(head * DV, (head + 1) * DV)
        gate = gate_ref[:, place].astype(f32)
        gating[:, place] = gain * (gate / (1.0 + jnp.exp(-gate)))

    def state_copy(head, target):
        return pltpu.make_async_remote_copy(
            src_ref=leaving.at[target], dst_ref=state.at[head],
            send_sem=state_send.at[target], recv_sem=state_recv.at[head],
            device_id={"ctx": target}, device_id_type=MESH,
        )

    @pl.when(me == 0)
    def _():
        state[...] = jnp.zeros_like(state)

    @pl.when(owner)
    def _():
        arrived[pl.ds(me, 1)] = map_ref[pl.ds(my_head, 1)]
        for step in range(n - 1):
            @pl.when(me != step)
            def _():
                map_copy(0, step, step).wait_recv()

        current = arrived[0, :, DK:].astype(f32)
        for step in range(n - 1):
            if step > 0:
                high = current.astype(bf16)
                low = (current - high.astype(f32)).astype(bf16)
                turned = mm(arrived[step, :, :DK], jnp.concatenate([high, low], axis=1))
                current = turned[:, :DV] + turned[:, DV:] + arrived[step, :, DK:].astype(f32)
            leaving[step + 1] = current.astype(bf16)

            @pl.when(me != step + 1)
            def _():
                state_copy(my_head, step + 1).start()

        @pl.when(me > 0)
        def _():
            state[pl.ds(my_head, 1)] = leaving[pl.ds(me, 1)]

    for head in range(heads):
        @pl.when((me > 0) & (me != head * apart))
        def _():
            state_copy(head, 0).wait_recv()

    ones = jnp.ones((DV, DV), bf16)
    for head in range(heads):
        place = slice(head * DV, (head + 1) * DV)
        core = mm(read_ref[:, place], state[head]) + own_ref[:, place]
        square_mean = mm((core * core).astype(bf16), ones) * (1.0 / DV)
        normed[:, place] = (core * lax.rsqrt(square_mean + 1e-06) * gating[:, place]).astype(bf16)

    for head in range(heads):
        @pl.when((me != head * apart) & (me < n - 1))
        def _():
            map_copy(head, me, head * apart).wait_send()

    for target in range(1, n):
        @pl.when(owner & (me != target))
        def _():
            state_copy(my_head, target).wait_send()


def sum_kernel(
    groups, normed, weight, out_ref, part, out_r, out_l, in_r, in_l, send_r, recv_r, send_l, recv_l
):
    chunks, _, rows, width = part.shape
    spot = lax.axis_index("tp")
    after, before = lax.rem(spot + 1, groups), lax.rem(spot + groups - 1, groups)
    barrier = pltpu.get_barrier_semaphore()

    @pl.when(spot > 0)
    def _():
        pl.semaphore_signal(barrier, inc=1, device_id={"tp": before}, device_id_type=MESH)

    @pl.when(spot < groups - 1)
    def _():
        pl.semaphore_signal(barrier, inc=1, device_id={"tp": after}, device_id_type=MESH)

    peers = (spot > 0).astype(jnp.int32) + (spot < groups - 1).astype(jnp.int32)
    pl.semaphore_wait(barrier, peers)

    def right_copy(source, c, target):
        return pltpu.make_async_remote_copy(
            src_ref=source.at[c, target], dst_ref=in_r.at[c, target],
            send_sem=send_r.at[c, target], recv_sem=recv_r.at[c, target],
            device_id={"tp": after}, device_id_type=MESH,
        )

    def left_copy(source, c, target):
        return pltpu.make_async_remote_copy(
            src_ref=source.at[c, target], dst_ref=in_l.at[c, target],
            send_sem=send_l.at[c, target], recv_sem=recv_l.at[c, target],
            device_id={"tp": before}, device_id_type=MESH,
        )

    @pl.when(spot == 0)
    def _():
        in_r[:, 0] = jnp.zeros_like(in_r[:, 0])

    @pl.when(spot == groups - 1)
    def _():
        in_l[:, groups - 1] = jnp.zeros_like(in_l[:, groups - 1])

    to_right = [(c, target) for c in range(chunks) for target in range(groups - 1, 0, -1)]
    to_left = [(c, target) for c in range(chunks) for target in range(groups - 1)]
    window = 2

    def feed(copy, order, c):
        for i, unit in enumerate(order):
            if unit[0] == c:
                if i >= window:
                    copy(part, *order[i - window]).wait_send()
                copy(part, *unit).start()

    for c in range(chunks):
        product = mm(normed[...], weight[:, c * width : (c + 1) * width]).astype(bf16)
        part[c] = product.reshape(groups, rows, width)

        @pl.when(spot == 0)
        def _():
            feed(right_copy, to_right, c)

        @pl.when(spot == groups - 1)
        def _():
            feed(left_copy, to_left, c)

    for c in range(chunks):
        def relay(step, carry):
            far = groups - 1 - step

            @pl.when((spot > 0) & (far > spot))
            def _():
                right_copy(part, c, far).wait_recv()
                out_r[c, far] = (in_r[c, far].astype(f32) + part[c, far].astype(f32)).astype(bf16)
                right_copy(out_r, c, far).start()

            @pl.when((spot < groups - 1) & (step < spot))
            def _():
                left_copy(part, c, step).wait_recv()
                out_l[c, step] = (in_l[c, step].astype(f32) + part[c, step].astype(f32)).astype(bf16)
                left_copy(out_l, c, step).start()

            return carry

        lax.fori_loop(0, groups - 1, relay, 0)

    for c in range(chunks):
        @pl.when(spot > 0)
        def _():
            right_copy(part, c, spot).wait_recv()

        @pl.when(spot < groups - 1)
        def _():
            left_copy(part, c, spot).wait_recv()

        mixed = part[c, spot].astype(f32) + in_r[c, spot].astype(f32) + in_l[c, spot].astype(f32)
        out_ref[:, c * width : (c + 1) * width] = mixed.astype(bf16)

    for c in range(chunks):
        def drain(target, carry):
            @pl.when((target > spot) & (spot > 0))
            def _():
                right_copy(part, c, target).wait_send()

            @pl.when((target < spot) & (spot < groups - 1))
            def _():
                left_copy(part, c, target).wait_send()

            return carry

        lax.fori_loop(0, groups, drain, 0)

    @pl.when(spot == 0)
    def _():
        for unit in to_right[-window:]:
            right_copy(part, *unit).wait_send()

    @pl.when(spot == groups - 1)
    def _():
        for unit in to_left[-window:]:
            left_copy(part, *unit).wait_send()


def local(n, groups, queries, key_vectors, value_vectors, output_gate, write_rate, log_decay, norm_gain, out_weight):
    tokens = queries.shape[0]
    heads = value_vectors.shape[1] // DV
    features, model = out_weight.shape
    rows = tokens // groups
    chunks = 4
    width = model // chunks
    piece = pltpu.VMEM((chunks, groups, rows, width), bf16)
    dma = pltpu.SemaphoreType.DMA
    inputs = (
        queries, key_vectors, value_vectors, output_gate,
        write_rate.T, log_decay.T, norm_gain.reshape(1, DV),
    )
    normed = pl.pallas_call(
        functools.partial(layer_kernel, n),
        in_specs=[pl.BlockSpec(memory_space=pl.ANY)] * len(inputs),
        out_specs=pl.BlockSpec(memory_space=pltpu.VMEM),
        out_shape=jax.ShapeDtypeStruct((tokens, features), bf16),
        scratch_shapes=[pltpu.VMEM(array.shape, array.dtype) for array in inputs] + [
            pltpu.VMEM((heads, DK, DK + DV), bf16),
            pltpu.VMEM((tokens, features), bf16),
            pltpu.VMEM((tokens, features), f32),
            pltpu.VMEM((tokens, features), f32),
            pltpu.VMEM((2, 128, tokens), f32),
            pltpu.VMEM((heads, tokens, tokens), bf16),
            pltpu.VMEM((heads, tokens, DK + DV), bf16),
            pltpu.VMEM((n, DK, DK + DV), bf16),
            pltpu.VMEM((n, DK, DV), bf16),
            pltpu.VMEM((heads, DK, DV), bf16),
            dma((len(inputs),)), dma((heads,)), dma((n,)), dma((n,)), dma((heads,)),
        ],
        compiler_params=pltpu.CompilerParams(
            collective_id=0, has_side_effects=True, vmem_limit_bytes=56 * 2**20
        ),
    )(*inputs)
    vmem = pl.BlockSpec(memory_space=pltpu.VMEM)
    return pl.pallas_call(
        functools.partial(sum_kernel, groups),
        in_specs=[vmem, vmem],
        out_specs=vmem,
        out_shape=jax.ShapeDtypeStruct((rows, model), bf16),
        scratch_shapes=[
            piece, piece, piece, piece, piece,
            dma((chunks, groups)), dma((chunks, groups)), dma((chunks, groups)), dma((chunks, groups)),
        ],
        compiler_params=pltpu.CompilerParams(
            collective_id=1, has_side_effects=True, vmem_limit_bytes=32 * 2**20
        ),
    )(normed, out_weight)


def solution(mesh):
    placed = (
        P("ctx", "tp"),
        P("ctx", "tp"),
        P("ctx", "tp"),
        P("ctx", "tp"),
        P("ctx", "tp"),
        P("ctx", "tp"),
        P(),
        P("tp", None),
    )
    body = functools.partial(local, mesh.shape["ctx"], mesh.shape["tp"])
    return jax.shard_map(
        body, mesh=mesh, in_specs=placed, out_specs=P(("ctx", "tp"), None), check_vma=False
    )
```

```python
import functools

import jax
import jax.numpy as jnp
from jax import lax
from jax.experimental import pallas as pl
from jax.experimental.pallas import tpu as pltpu
from jax.sharding import PartitionSpec as P

DK = 128
DV = 128
MESH = pl.DeviceIdType.MESH
f32, bf16 = jnp.float32, jnp.bfloat16


def mm(left, right):
    return jnp.dot(left, right, preferred_element_type=f32)


def mm_rows(left, right):
    return lax.dot_general(left, right, (((1,), (1,)), ((), ())), preferred_element_type=f32)


def mm_cols(left, right):
    return lax.dot_general(left, right, (((0,), (0,)), ((), ())), preferred_element_type=f32)


def unit_lower_inverses(lowers):
    size = lowers[0].shape[0]
    row = lax.broadcasted_iota(jnp.int32, (size, size), 0)
    col = lax.broadcasted_iota(jnp.int32, (size, size), 1)
    apart = row ^ col
    eye = jnp.where(row == col, 1.0, 0.0)
    inverses = [eye - jnp.where(apart == 1, lower, 0.0) for lower in lowers]
    step = 2
    while step < size:
        coupling = (apart >= step) & (apart < 2 * step)
        rounded = [inverse.astype(bf16) for inverse in inverses]
        inner = [
            mm(jnp.where(coupling, lower, 0.0).astype(bf16), r).astype(bf16)
            for lower, r in zip(lowers, rounded)
        ]
        inverses = [inverse - mm(r, i) for inverse, r, i in zip(inverses, rounded, inner)]
        step *= 2
    rounded = [inverse.astype(bf16) for inverse in inverses]
    highs = [lower.astype(bf16) for lower in lowers]
    lows = [(lower - high.astype(f32)).astype(bf16) for lower, high in zip(lowers, highs)]
    residuals = [
        (eye - r.astype(f32) - mm(high, r) - mm(low, r)).astype(bf16)
        for high, low, r in zip(highs, lows, rounded)
    ]
    return [r.astype(f32) + mm(r, residual) for r, residual in zip(rounded, residuals)]


def square_sums(source, key_heads, sharing):
    lane = lax.broadcasted_iota(jnp.int32, (DK, 128), 1)
    sums = 0.0
    for group in range(key_heads):
        mine = (lane >= group * sharing) & (lane < (group + 1) * sharing)
        chosen = jnp.where(mine, 1.0, 0.0).astype(bf16)
        values = source[:, group * DK : (group + 1) * DK].astype(f32)
        squares = values * values
        high = squares.astype(bf16)
        sums = sums + mm(high, chosen) + mm((squares - high.astype(f32)).astype(bf16), chosen)
    return sums


def prepare(key_heads, sharing, q_ref, k_ref, rate_ref, decay_ref, turn_ref, scores_ref):
    tokens, heads = q_ref.shape[0], rate_ref.shape[0]
    half = tokens // 2
    row = lax.broadcasted_iota(jnp.int32, (tokens, tokens), 0)
    col = lax.broadcasted_iota(jnp.int32, (tokens, tokens), 1)
    upper = jnp.where(row <= col, 1.0, 0.0)
    total_rows = jnp.dot(
        decay_ref[...], upper, precision=lax.Precision.HIGHEST, preferred_element_type=f32
    )
    rate_rows = rate_ref[...]
    turn_ref[...] = jnp.zeros_like(turn_ref)
    turn_ref[0, :heads] = rate_rows
    turn_ref[1, :heads] = total_rows
    rate, total = turn_ref[0].T, turn_ref[1].T
    key_scale = lax.rsqrt(square_sums(k_ref, key_heads, sharing) + 1e-06)
    query_scale = lax.rsqrt(square_sums(q_ref, key_heads, sharing) + 1e-06)
    key_rows = key_scale.T[:heads]
    erase_rows = rate_rows * jnp.exp(total_rows) * key_rows
    closing = total[tokens - 1 :, :]
    fade = jnp.exp(closing)
    write_scale = jnp.exp(closing - total) * key_scale
    strength = rate * key_scale

    half_row = lax.broadcasted_iota(jnp.int32, (half, half), 0)
    half_col = lax.broadcasted_iota(jnp.int32, (half, half), 1)
    inclusive, strict = half_row >= half_col, half_row > half_col
    parts = []
    for group in range(key_heads):
        key_place = slice(group * DK, (group + 1) * DK)
        queries, keys = q_ref[:, key_place], k_ref[:, key_place]
        gram = mm_rows(keys, keys)
        reads = mm_rows(queries, keys)
        for head in range(group * sharing, (group + 1) * sharing):
            here = slice(head, head + 1)
            total_row, key_row = total_rows[here], key_rows[here]

            def spread(rows, cols):
                return jnp.exp(total[rows, here] - total_row[:, cols])

            top, low = slice(0, half), slice(half, tokens)
            ratio_a = jnp.where(inclusive, spread(top, top), 0.0) * key_row[:, top]
            ratio_b = jnp.where(inclusive, spread(low, low), 0.0) * key_row[:, low]
            ratio_c = spread(low, top) * key_row[:, top]
            scores_ref[head, :half, :half] = (reads[top, top] * ratio_a).astype(bf16)
            scores_ref[head, half:, :half] = (reads[low, top] * ratio_c).astype(bf16)
            scores_ref[head, half:, half:] = (reads[low, low] * ratio_b).astype(bf16)
            lower_a = jnp.where(strict, gram[top, top] * ratio_a * strength[top, here], 0.0)
            lower_b = jnp.where(strict, gram[low, low] * ratio_b * strength[low, here], 0.0)
            lower_c = (gram[low, top] * ratio_c * strength[low, here]).astype(bf16)
            parts.append((
                rate_rows[here], erase_rows[here], write_scale[:, here], fade[:, here],
                jnp.exp(total[:, here]), query_scale[:, here], lower_a, lower_b, lower_c,
            ))
    return parts


def invert(parts):
    inverses = unit_lower_inverses([block for part in parts for block in part[6:8]])
    firsts, seconds = inverses[0::2], inverses[1::2]
    inner = [mm(part[8], first.astype(bf16)).astype(bf16) for part, first in zip(parts, firsts)]
    corners = [-mm(second.astype(bf16), i) for second, i in zip(seconds, inner)]
    return list(zip(firsts, seconds, corners))


def head_map(part, blocks, keys, values, map_ref, both_ref):
    rate_row, erase_row, write_scale, fade = part[:4]
    first, second, corner = blocks
    half = first.shape[0]
    key_row = lax.broadcasted_iota(jnp.int32, (DK, DK), 0)
    key_col = lax.broadcasted_iota(jnp.int32, (DK, DK), 1)

    def solved(scale_row, right):
        left_scale, right_scale = scale_row[:, :half], scale_row[:, half:]
        top = mm((first * left_scale).astype(bf16), right[:half])
        bottom = mm((corner * left_scale).astype(bf16), right[:half])
        bottom += mm((second * right_scale).astype(bf16), right[half:])
        return jnp.concatenate([top, bottom], axis=0)

    both = jnp.concatenate([solved(erase_row, keys), solved(rate_row, values)], axis=1)
    both_ref[...] = both.astype(bf16)
    summary = mm_cols(keys, (both * write_scale).astype(bf16))
    moved = jnp.where(key_row == key_col, fade, 0.0) - summary[:, :DK]
    map_ref[:, :DK] = moved.astype(bf16)
    map_ref[:, DK:] = summary[:, DK:].astype(bf16)


def layer_kernel(
    n, groups, q_hbm, k_hbm, v_hbm, gate_hbm, rate_hbm, decay_hbm, gain_hbm, weight_hbm, out_ref,
    q_ref, k_ref, v_ref, gate_ref, rate_ref, decay_ref, gain_ref, weight,
    map_ref, read_ref, own_ref, gating, turn_ref, scores_ref, both_ref,
    arrived, leaving, state, normed, part, out_r, out_l, in_r, in_l,
    load_sem, map_send, map_recv, state_send, state_recv,
    send_r, recv_r, send_l, recv_l,
):
    heads = map_ref.shape[0]
    apart = n // heads
    chunks, _, rows, width = part.shape
    me, spot = lax.axis_index("ctx"), lax.axis_index("tp")
    my_head = me // apart
    owner = lax.rem(me, apart) == 0

    loads = [
        pltpu.make_async_copy(source, target, load_sem.at[i])
        for i, (source, target) in enumerate((
            (k_hbm, k_ref), (q_hbm, q_ref), (rate_hbm, rate_ref), (decay_hbm, decay_ref),
            (v_hbm, v_ref), (gain_hbm, gain_ref), (gate_hbm, gate_ref), (weight_hbm, weight),
        ))
    ]
    for load in loads[:4]:
        load.start()

    barrier = pltpu.get_barrier_semaphore()
    for other in range(n):
        @pl.when(me != other)
        def _():
            pl.semaphore_signal(barrier, inc=1, device_id={"ctx": other}, device_id_type=MESH)

    after, before = lax.rem(spot + 1, groups), lax.rem(spot + groups - 1, groups)

    @pl.when(spot > 0)
    def _():
        pl.semaphore_signal(barrier, inc=1, device_id={"tp": before}, device_id_type=MESH)

    @pl.when(spot < groups - 1)
    def _():
        pl.semaphore_signal(barrier, inc=1, device_id={"tp": after}, device_id_type=MESH)

    peers = (spot > 0).astype(jnp.int32) + (spot < groups - 1).astype(jnp.int32)
    def map_copy(head, slot, target):
        return pltpu.make_async_remote_copy(
            src_ref=map_ref.at[head], dst_ref=arrived.at[slot],
            send_sem=map_send.at[head], recv_sem=map_recv.at[slot],
            device_id={"ctx": target}, device_id_type=MESH,
        )

    key_heads = k_ref.shape[1] // DK
    sharing = heads // key_heads
    for load in loads[:4]:
        load.wait()
    for load in loads[4:]:
        load.start()
    parts = prepare(key_heads, sharing, q_ref, k_ref, rate_ref, decay_ref, turn_ref, scores_ref)
    blocks = invert(parts)
    loads[4].wait()
    for head in range(heads):
        place = slice(head * DV, (head + 1) * DV)
        group = head // sharing
        keys = k_ref[:, group * DK : (group + 1) * DK]
        head_map(
            parts[head], blocks[head], keys, v_ref[:, place], map_ref.at[head], both_ref.at[head]
        )
        if head == 0:
            pl.semaphore_wait(barrier, n - 1 + peers)

        @pl.when((me != head * apart) & (me < n - 1))
        def _():
            map_copy(head, me, head * apart).start()

    half = q_ref.shape[0] // 2
    for head in range(heads):
        place = slice(head * DV, (head + 1) * DV)
        group = head // sharing
        queries = q_ref[:, group * DK : (group + 1) * DK].astype(f32)
        decayed, query_scale = parts[head][4:6]
        top = mm(scores_ref[head, :half, :half], both_ref[head, :half])
        low = mm(scores_ref[head, half:], both_ref[head])
        seen = jnp.concatenate([top, low], axis=0)
        read_ref[:, place] = ((decayed * queries - seen[:, :DK]) * query_scale).astype(bf16)
        own_ref[:, place] = seen[:, DK:] * query_scale

    for load in loads[5:]:
        load.wait()
    gain = gain_ref[...]
    for head in range(heads):
        place = slice(head * DV, (head + 1) * DV)
        gate = gate_ref[:, place].astype(f32)
        gating[:, place] = gain * (gate / (1.0 + jnp.exp(-gate)))

    def state_copy(head, target):
        return pltpu.make_async_remote_copy(
            src_ref=leaving.at[target], dst_ref=state.at[head],
            send_sem=state_send.at[target], recv_sem=state_recv.at[head],
            device_id={"ctx": target}, device_id_type=MESH,
        )

    @pl.when(me == 0)
    def _():
        state[...] = jnp.zeros_like(state)

    @pl.when(owner)
    def _():
        arrived[pl.ds(me, 1)] = map_ref[pl.ds(my_head, 1)]
        for step in range(n - 1):
            @pl.when(me != step)
            def _():
                map_copy(0, step, step).wait_recv()

        current = arrived[0, :, DK:].astype(f32)
        for step in range(n - 1):
            if step > 0:
                high = current.astype(bf16)
                low = (current - high.astype(f32)).astype(bf16)
                turned = mm(arrived[step, :, :DK], jnp.concatenate([high, low], axis=1))
                current = turned[:, :DV] + turned[:, DV:] + arrived[step, :, DK:].astype(f32)
            leaving[step + 1] = current.astype(bf16)

            @pl.when(me != step + 1)
            def _():
                state_copy(my_head, step + 1).start()

        @pl.when(me > 0)
        def _():
            state[pl.ds(my_head, 1)] = leaving[pl.ds(me, 1)]

    for head in range(heads):
        @pl.when((me > 0) & (me != head * apart))
        def _():
            state_copy(head, 0).wait_recv()

    ones = jnp.ones((DV, DV), bf16)
    for head in range(heads):
        place = slice(head * DV, (head + 1) * DV)
        core = mm(read_ref[:, place], state[head]) + own_ref[:, place]
        square_mean = mm((core * core).astype(bf16), ones) * (1.0 / DV)
        normed[:, place] = (core * lax.rsqrt(square_mean + 1e-06) * gating[:, place]).astype(bf16)

    def right_copy(source, c, target):
        return pltpu.make_async_remote_copy(
            src_ref=source.at[c, target], dst_ref=in_r.at[c, target],
            send_sem=send_r.at[c, target], recv_sem=recv_r.at[c, target],
            device_id={"tp": after}, device_id_type=MESH,
        )

    def left_copy(source, c, target):
        return pltpu.make_async_remote_copy(
            src_ref=source.at[c, target], dst_ref=in_l.at[c, target],
            send_sem=send_l.at[c, target], recv_sem=recv_l.at[c, target],
            device_id={"tp": before}, device_id_type=MESH,
        )

    @pl.when(spot == 0)
    def _():
        in_r[:, 0] = jnp.zeros_like(in_r[:, 0])

    @pl.when(spot == groups - 1)
    def _():
        in_l[:, groups - 1] = jnp.zeros_like(in_l[:, groups - 1])

    units = (groups - 1) * chunks

    def right_unit(u):
        return u % chunks, groups - 1 - u // chunks

    def left_unit(u):
        return u % chunks, u // chunks

    for c in range(chunks):
        product = mm(normed[...], weight[:, c * width : (c + 1) * width]).astype(bf16)
        part[c] = product.reshape(groups, rows, width)

        @pl.when(spot == 0)
        def _():
            right_copy(part, *right_unit(c)).start()

        @pl.when(spot == groups - 1)
        def _():
            left_copy(part, *left_unit(c)).start()

    @pl.when(spot == 0)
    def _():
        for u in range(chunks, units):
            right_copy(part, *right_unit(u - chunks)).wait_send()
            right_copy(part, *right_unit(u)).start()

    @pl.when(spot == groups - 1)
    def _():
        for u in range(chunks, units):
            left_copy(part, *left_unit(u - chunks)).wait_send()
            left_copy(part, *left_unit(u)).start()

    lag = 2

    def relay(time, carry):
        u = time - lag * (spot - 1)
        c, target = u % chunks, groups - 1 - u // chunks

        @pl.when((spot > 0) & (u >= 0) & (target > spot))
        def _():
            right_copy(part, c, target).wait_recv()
            out_r[c, target] = (in_r[c, target].astype(f32) + part[c, target].astype(f32)).astype(bf16)
            right_copy(out_r, c, target).start()

        v = time - lag * (groups - 2 - spot)
        d, goal = v % chunks, v // chunks

        @pl.when((spot < groups - 1) & (v >= 0) & (goal < spot))
        def _():
            left_copy(part, d, goal).wait_recv()
            out_l[d, goal] = (in_l[d, goal].astype(f32) + part[d, goal].astype(f32)).astype(bf16)
            left_copy(out_l, d, goal).start()

        return carry

    lax.fori_loop(0, units + lag * (groups - 2), relay, 0)

    for c in range(chunks):
        @pl.when(spot > 0)
        def _():
            right_copy(part, c, spot).wait_recv()

        @pl.when(spot < groups - 1)
        def _():
            left_copy(part, c, spot).wait_recv()

        mixed = part[c, spot].astype(f32) + in_r[c, spot].astype(f32) + in_l[c, spot].astype(f32)
        out_ref[:, c * width : (c + 1) * width] = mixed.astype(bf16)

    for head in range(heads):
        @pl.when((me != head * apart) & (me < n - 1))
        def _():
            map_copy(head, me, head * apart).wait_send()

    for target in range(1, n):
        @pl.when(owner & (me != target))
        def _():
            state_copy(my_head, target).wait_send()

    for c in range(chunks):
        def drain(target, carry):
            @pl.when((target > spot) & (spot > 0))
            def _():
                right_copy(part, c, target).wait_send()

            @pl.when((target < spot) & (spot < groups - 1))
            def _():
                left_copy(part, c, target).wait_send()

            return carry

        lax.fori_loop(0, groups, drain, 0)

    @pl.when(spot == 0)
    def _():
        for u in range(units - chunks, units):
            right_copy(part, *right_unit(u)).wait_send()

    @pl.when(spot == groups - 1)
    def _():
        for u in range(units - chunks, units):
            left_copy(part, *left_unit(u)).wait_send()


def local(n, groups, queries, key_vectors, value_vectors, output_gate, write_rate, log_decay, norm_gain, out_weight):
    tokens = queries.shape[0]
    heads = value_vectors.shape[1] // DV
    features, model = out_weight.shape
    rows = tokens // groups
    chunks = 4
    width = model // chunks
    piece = pltpu.VMEM((chunks, groups, rows, width), bf16)
    dma = pltpu.SemaphoreType.DMA
    inputs = (
        queries, key_vectors, value_vectors, output_gate,
        write_rate.T, log_decay.T, norm_gain.reshape(1, DV), out_weight,
    )
    return pl.pallas_call(
        functools.partial(layer_kernel, n, groups),
        in_specs=[pl.BlockSpec(memory_space=pl.ANY)] * len(inputs),
        out_specs=pl.BlockSpec(memory_space=pltpu.VMEM),
        out_shape=jax.ShapeDtypeStruct((rows, model), bf16),
        scratch_shapes=[pltpu.VMEM(array.shape, array.dtype) for array in inputs] + [
            pltpu.VMEM((heads, DK, DK + DV), bf16),
            pltpu.VMEM((tokens, features), bf16),
            pltpu.VMEM((tokens, features), f32),
            pltpu.VMEM((tokens, features), f32),
            pltpu.VMEM((2, 128, tokens), f32),
            pltpu.VMEM((heads, tokens, tokens), bf16),
            pltpu.VMEM((heads, tokens, DK + DV), bf16),
            pltpu.VMEM((n, DK, DK + DV), bf16),
            pltpu.VMEM((n, DK, DV), bf16),
            pltpu.VMEM((heads, DK, DV), bf16),
            pltpu.VMEM((tokens, features), bf16),
            piece, piece, piece, piece, piece,
            dma((len(inputs),)), dma((heads,)), dma((n,)), dma((n,)), dma((heads,)),
            dma((chunks, groups)), dma((chunks, groups)), dma((chunks, groups)), dma((chunks, groups)),
        ],
        compiler_params=pltpu.CompilerParams(
            collective_id=0, has_side_effects=True, vmem_limit_bytes=56 * 2**20
        ),
    )(*inputs)


def solution(mesh):
    placed = (
        P("ctx", "tp"),
        P("ctx", "tp"),
        P("ctx", "tp"),
        P("ctx", "tp"),
        P("ctx", "tp"),
        P("ctx", "tp"),
        P(),
        P("tp", None),
    )
    body = functools.partial(local, mesh.shape["ctx"], mesh.shape["tp"])
    return jax.shard_map(
        body, mesh=mesh, in_specs=placed, out_specs=P(("ctx", "tp"), None), check_vma=False
    )
```

```python
import functools

import jax
import jax.numpy as jnp
from jax import lax
from jax.experimental import pallas as pl
from jax.experimental.pallas import tpu as pltpu
from jax.sharding import PartitionSpec as P

DK = 128
DV = 128
MESH = pl.DeviceIdType.MESH
f32, bf16 = jnp.float32, jnp.bfloat16


def mm(left, right):
    return jnp.dot(left, right, preferred_element_type=f32)


def unit_lower_inverses(lowers):
    size = lowers[0].shape[0]
    row = lax.broadcasted_iota(jnp.int32, (size, size), 0)
    col = lax.broadcasted_iota(jnp.int32, (size, size), 1)
    apart = row ^ col
    eye = jnp.where(row == col, 1.0, 0.0)
    inverses = [eye - jnp.where(apart == 1, lower, 0.0) for lower in lowers]
    step = 2
    while step < size:
        coupling = (apart >= step) & (apart < 2 * step)
        rounded = [inverse.astype(bf16) for inverse in inverses]
        inner = [
            mm(jnp.where(coupling, lower, 0.0).astype(bf16), r).astype(bf16)
            for lower, r in zip(lowers, rounded)
        ]
        inverses = [inverse - mm(r, i) for inverse, r, i in zip(inverses, rounded, inner)]
        step *= 2
    rounded = [inverse.astype(bf16) for inverse in inverses]
    highs = [lower.astype(bf16) for lower in lowers]
    lows = [(lower - high.astype(f32)).astype(bf16) for lower, high in zip(lowers, highs)]
    residuals = [
        (eye - r.astype(f32) - mm(high, r) - mm(low, r)).astype(bf16)
        for high, low, r in zip(highs, lows, rounded)
    ]
    return [r.astype(f32) + mm(r, residual) for r, residual in zip(rounded, residuals)]


def square_sums(source, key_heads, sharing):
    lane = lax.broadcasted_iota(jnp.int32, (DK, 128), 1)
    sums = 0.0
    for group in range(key_heads):
        mine = (lane >= group * sharing) & (lane < (group + 1) * sharing)
        chosen = jnp.where(mine, 1.0, 0.0).astype(bf16)
        values = source[:, group * DK : (group + 1) * DK].astype(f32)
        squares = values * values
        high = squares.astype(bf16)
        sums = sums + mm(high, chosen) + mm((squares - high.astype(f32)).astype(bf16), chosen)
    return sums


def prepare(key_heads, sharing, q_ref, k_ref, rate_ref, decay_ref, turn_ref, turned_ref, scores_ref):
    tokens, heads = q_ref.shape[0], rate_ref.shape[0]
    half = tokens // 2
    row = lax.broadcasted_iota(jnp.int32, (tokens, tokens), 0)
    col = lax.broadcasted_iota(jnp.int32, (tokens, tokens), 1)
    upper = jnp.where(row <= col, 1.0, 0.0)
    total_rows = jnp.dot(
        decay_ref[...], upper, precision=lax.Precision.HIGHEST, preferred_element_type=f32
    )
    rate_rows = rate_ref[...]
    turn_ref[...] = jnp.zeros_like(turn_ref)
    turn_ref[0, :heads] = rate_rows
    turn_ref[1, :heads] = total_rows
    rate, total = turn_ref[0].T, turn_ref[1].T
    key_scale = lax.rsqrt(square_sums(k_ref, key_heads, sharing) + 1e-06)
    query_scale = lax.rsqrt(square_sums(q_ref, key_heads, sharing) + 1e-06)
    key_rows = key_scale.T[:heads]
    erase_rows = rate_rows * jnp.exp(total_rows) * key_rows
    closing = total[tokens - 1 :, :]
    fade = jnp.exp(closing)
    write_scale = jnp.exp(closing - total) * key_scale
    strength = rate * key_scale

    half_row = lax.broadcasted_iota(jnp.int32, (half, half), 0)
    half_col = lax.broadcasted_iota(jnp.int32, (half, half), 1)
    inclusive, strict = half_row >= half_col, half_row > half_col
    parts = []
    for group in range(key_heads):
        key_place = slice(group * DK, (group + 1) * DK)
        queries, keys = q_ref[:, key_place], k_ref[:, key_place]
        turned_keys = keys.T
        turned_ref[group] = turned_keys
        gram = mm(keys, turned_keys)
        reads = mm(queries, turned_keys)
        for head in range(group * sharing, (group + 1) * sharing):
            here = slice(head, head + 1)
            total_row, key_row = total_rows[here], key_rows[here]

            def spread(rows, cols):
                return jnp.exp(total[rows, here] - total_row[:, cols])

            top, low = slice(0, half), slice(half, tokens)
            ratio_a = jnp.where(inclusive, spread(top, top), 0.0) * key_row[:, top]
            ratio_b = jnp.where(inclusive, spread(low, low), 0.0) * key_row[:, low]
            ratio_c = spread(low, top) * key_row[:, top]
            scores_ref[head, :half, :half] = (reads[top, top] * ratio_a).astype(bf16)
            scores_ref[head, half:, :half] = (reads[low, top] * ratio_c).astype(bf16)
            scores_ref[head, half:, half:] = (reads[low, low] * ratio_b).astype(bf16)
            lower_a = jnp.where(strict, gram[top, top] * ratio_a * strength[top, here], 0.0)
            lower_b = jnp.where(strict, gram[low, low] * ratio_b * strength[low, here], 0.0)
            lower_c = (gram[low, top] * ratio_c * strength[low, here]).astype(bf16)
            parts.append((
                rate_rows[here], erase_rows[here], write_scale[:, here], fade[:, here],
                jnp.exp(total[:, here]), query_scale[:, here], lower_a, lower_b, lower_c,
            ))
    return parts


def invert(parts):
    inverses = unit_lower_inverses([block for part in parts for block in part[6:8]])
    firsts, seconds = inverses[0::2], inverses[1::2]
    inner = [mm(part[8], first.astype(bf16)).astype(bf16) for part, first in zip(parts, firsts)]
    corners = [-mm(second.astype(bf16), i) for second, i in zip(seconds, inner)]
    return list(zip(firsts, seconds, corners))


def head_map(part, blocks, keys, turned_keys, values, map_ref, both_ref):
    rate_row, erase_row, write_scale, fade = part[:4]
    first, second, corner = blocks
    half = first.shape[0]
    key_row = lax.broadcasted_iota(jnp.int32, (DK, DK), 0)
    key_col = lax.broadcasted_iota(jnp.int32, (DK, DK), 1)

    def solved(scale_row, right):
        left_scale, right_scale = scale_row[:, :half], scale_row[:, half:]
        top = mm((first * left_scale).astype(bf16), right[:half])
        bottom = mm((corner * left_scale).astype(bf16), right[:half])
        bottom += mm((second * right_scale).astype(bf16), right[half:])
        return jnp.concatenate([top, bottom], axis=0)

    both = jnp.concatenate([solved(erase_row, keys), solved(rate_row, values)], axis=1)
    both_ref[...] = both.astype(bf16)
    summary = mm(turned_keys, (both * write_scale).astype(bf16))
    moved = jnp.where(key_row == key_col, fade, 0.0) - summary[:, :DK]
    map_ref[:, :DK] = moved.astype(bf16)
    map_ref[:, DK:] = summary[:, DK:].astype(bf16)


def layer_kernel(
    n, groups, q_hbm, k_hbm, v_hbm, gate_hbm, rate_hbm, decay_hbm, gain_hbm, weight_hbm, out_ref,
    q_ref, k_ref, v_ref, gate_ref, rate_ref, decay_ref, gain_ref, weight,
    map_ref, read_ref, own_ref, gating, turn_ref, turned_ref, scores_ref, both_ref,
    arrived, leaving, state, normed, part, out_r, out_l, in_r, in_l,
    load_sem, map_send, map_recv, state_send, state_recv,
    send_r, recv_r, send_l, recv_l,
):
    heads = map_ref.shape[0]
    apart = n // heads
    chunks, _, rows, width = part.shape
    me, spot = lax.axis_index("ctx"), lax.axis_index("tp")
    my_head = me // apart
    owner = lax.rem(me, apart) == 0

    loads = [
        pltpu.make_async_copy(source, target, load_sem.at[i])
        for i, (source, target) in enumerate((
            (k_hbm, k_ref), (q_hbm, q_ref), (rate_hbm, rate_ref), (decay_hbm, decay_ref),
            (v_hbm, v_ref), (gain_hbm, gain_ref), (gate_hbm, gate_ref), (weight_hbm, weight),
        ))
    ]
    for load in loads[:4]:
        load.start()

    barrier = pltpu.get_barrier_semaphore()
    for other in range(n):
        @pl.when(me != other)
        def _():
            pl.semaphore_signal(barrier, inc=1, device_id={"ctx": other}, device_id_type=MESH)

    after, before = lax.rem(spot + 1, groups), lax.rem(spot + groups - 1, groups)

    @pl.when(spot > 0)
    def _():
        pl.semaphore_signal(barrier, inc=1, device_id={"tp": before}, device_id_type=MESH)

    @pl.when(spot < groups - 1)
    def _():
        pl.semaphore_signal(barrier, inc=1, device_id={"tp": after}, device_id_type=MESH)

    peers = (spot > 0).astype(jnp.int32) + (spot < groups - 1).astype(jnp.int32)
    def map_copy(head, slot, target):
        return pltpu.make_async_remote_copy(
            src_ref=map_ref.at[head], dst_ref=arrived.at[slot],
            send_sem=map_send.at[head], recv_sem=map_recv.at[slot],
            device_id={"ctx": target}, device_id_type=MESH,
        )

    key_heads = k_ref.shape[1] // DK
    sharing = heads // key_heads
    for load in loads[:4]:
        load.wait()
    for load in loads[4:]:
        load.start()
    parts = prepare(key_heads, sharing, q_ref, k_ref, rate_ref, decay_ref, turn_ref, turned_ref, scores_ref)
    blocks = invert(parts)
    loads[4].wait()
    together = min(4, heads)
    for start in range(0, heads, together):
        for head in range(start, start + together):
            place = slice(head * DV, (head + 1) * DV)
            group = head // sharing
            keys = k_ref[:, group * DK : (group + 1) * DK]
            head_map(
                parts[head], blocks[head], keys, turned_ref[group], v_ref[:, place],
                map_ref.at[head], both_ref.at[head],
            )
        if start == 0:
            pl.semaphore_wait(barrier, n - 1 + peers)
        for head in range(start, start + together):
            @pl.when((me != head * apart) & (me < n - 1))
            def _():
                map_copy(head, me, head * apart).start()

    half = q_ref.shape[0] // 2
    for head in range(heads):
        place = slice(head * DV, (head + 1) * DV)
        group = head // sharing
        queries = q_ref[:, group * DK : (group + 1) * DK].astype(f32)
        decayed, query_scale = parts[head][4:6]
        top = mm(scores_ref[head, :half, :half], both_ref[head, :half])
        low = mm(scores_ref[head, half:], both_ref[head])
        seen = jnp.concatenate([top, low], axis=0)
        read_ref[:, place] = ((decayed * queries - seen[:, :DK]) * query_scale).astype(bf16)
        own_ref[:, place] = seen[:, DK:] * query_scale

    for load in loads[5:]:
        load.wait()
    gain = gain_ref[...]
    for head in range(heads):
        place = slice(head * DV, (head + 1) * DV)
        gate = gate_ref[:, place].astype(f32)
        gating[:, place] = gain * (gate / (1.0 + jnp.exp(-gate)))

    def state_copy(head, target):
        return pltpu.make_async_remote_copy(
            src_ref=leaving.at[target], dst_ref=state.at[head],
            send_sem=state_send.at[target], recv_sem=state_recv.at[head],
            device_id={"ctx": target}, device_id_type=MESH,
        )

    @pl.when(me == 0)
    def _():
        state[...] = jnp.zeros_like(state)

    @pl.when(owner)
    def _():
        arrived[pl.ds(me, 1)] = map_ref[pl.ds(my_head, 1)]
        for step in range(n - 1):
            @pl.when(me != step)
            def _():
                map_copy(0, step, step).wait_recv()

        current = arrived[0, :, DK:].astype(f32)
        for step in range(n - 1):
            if step > 0:
                high = current.astype(bf16)
                low = (current - high.astype(f32)).astype(bf16)
                turned = mm(arrived[step, :, :DK], jnp.concatenate([high, low], axis=1))
                current = turned[:, :DV] + turned[:, DV:] + arrived[step, :, DK:].astype(f32)
            leaving[step + 1] = current.astype(bf16)

            @pl.when(me != step + 1)
            def _():
                state_copy(my_head, step + 1).start()

        @pl.when(me > 0)
        def _():
            state[pl.ds(my_head, 1)] = leaving[pl.ds(me, 1)]

    for head in range(heads):
        @pl.when((me > 0) & (me != head * apart))
        def _():
            state_copy(head, 0).wait_recv()

    ones = jnp.ones((DV, DV), bf16)
    for head in range(heads):
        place = slice(head * DV, (head + 1) * DV)
        core = mm(read_ref[:, place], state[head]) + own_ref[:, place]
        square_mean = mm((core * core).astype(bf16), ones) * (1.0 / DV)
        normed[:, place] = (core * lax.rsqrt(square_mean + 1e-06) * gating[:, place]).astype(bf16)

    def right_copy(source, c, target):
        return pltpu.make_async_remote_copy(
            src_ref=source.at[c, target], dst_ref=in_r.at[c, target],
            send_sem=send_r.at[c, target], recv_sem=recv_r.at[c, target],
            device_id={"tp": after}, device_id_type=MESH,
        )

    def left_copy(source, c, target):
        return pltpu.make_async_remote_copy(
            src_ref=source.at[c, target], dst_ref=in_l.at[c, target],
            send_sem=send_l.at[c, target], recv_sem=recv_l.at[c, target],
            device_id={"tp": before}, device_id_type=MESH,
        )

    @pl.when(spot == 0)
    def _():
        in_r[:, 0] = jnp.zeros_like(in_r[:, 0])

    @pl.when(spot == groups - 1)
    def _():
        in_l[:, groups - 1] = jnp.zeros_like(in_l[:, groups - 1])

    units = (groups - 1) * chunks

    def right_unit(u):
        return u % chunks, groups - 1 - u // chunks

    def left_unit(u):
        return u % chunks, u // chunks

    for c in range(chunks):
        product = mm(normed[...], weight[:, c * width : (c + 1) * width]).astype(bf16)
        part[c] = product.reshape(groups, rows, width)

        @pl.when(spot == 0)
        def _():
            right_copy(part, *right_unit(c)).start()

        @pl.when(spot == groups - 1)
        def _():
            left_copy(part, *left_unit(c)).start()

    @pl.when(spot == 0)
    def _():
        for u in range(chunks, units):
            right_copy(part, *right_unit(u - chunks)).wait_send()
            right_copy(part, *right_unit(u)).start()

    @pl.when(spot == groups - 1)
    def _():
        for u in range(chunks, units):
            left_copy(part, *left_unit(u - chunks)).wait_send()
            left_copy(part, *left_unit(u)).start()

    lag = 2

    def relay(time, carry):
        u = time - lag * (spot - 1)
        c, target = u % chunks, groups - 1 - u // chunks

        @pl.when((spot > 0) & (u >= 0) & (target > spot))
        def _():
            right_copy(part, c, target).wait_recv()
            out_r[c, target] = (in_r[c, target].astype(f32) + part[c, target].astype(f32)).astype(bf16)
            right_copy(out_r, c, target).start()

        v = time - lag * (groups - 2 - spot)
        d, goal = v % chunks, v // chunks

        @pl.when((spot < groups - 1) & (v >= 0) & (goal < spot))
        def _():
            left_copy(part, d, goal).wait_recv()
            out_l[d, goal] = (in_l[d, goal].astype(f32) + part[d, goal].astype(f32)).astype(bf16)
            left_copy(out_l, d, goal).start()

        return carry

    lax.fori_loop(0, units + lag * (groups - 2), relay, 0)

    for c in range(chunks):
        @pl.when(spot > 0)
        def _():
            right_copy(part, c, spot).wait_recv()

        @pl.when(spot < groups - 1)
        def _():
            left_copy(part, c, spot).wait_recv()

        mixed = part[c, spot].astype(f32) + in_r[c, spot].astype(f32) + in_l[c, spot].astype(f32)
        out_ref[:, c * width : (c + 1) * width] = mixed.astype(bf16)

    for head in range(heads):
        @pl.when((me != head * apart) & (me < n - 1))
        def _():
            map_copy(head, me, head * apart).wait_send()

    for target in range(1, n):
        @pl.when(owner & (me != target))
        def _():
            state_copy(my_head, target).wait_send()

    for c in range(chunks):
        def drain(target, carry):
            @pl.when((target > spot) & (spot > 0))
            def _():
                right_copy(part, c, target).wait_send()

            @pl.when((target < spot) & (spot < groups - 1))
            def _():
                left_copy(part, c, target).wait_send()

            return carry

        lax.fori_loop(0, groups, drain, 0)

    @pl.when(spot == 0)
    def _():
        for u in range(units - chunks, units):
            right_copy(part, *right_unit(u)).wait_send()

    @pl.when(spot == groups - 1)
    def _():
        for u in range(units - chunks, units):
            left_copy(part, *left_unit(u)).wait_send()


def local(n, groups, queries, key_vectors, value_vectors, output_gate, write_rate, log_decay, norm_gain, out_weight):
    tokens = queries.shape[0]
    heads = value_vectors.shape[1] // DV
    features, model = out_weight.shape
    rows = tokens // groups
    chunks = 4
    width = model // chunks
    piece = pltpu.VMEM((chunks, groups, rows, width), bf16)
    dma = pltpu.SemaphoreType.DMA
    inputs = (
        queries, key_vectors, value_vectors, output_gate,
        write_rate.T, log_decay.T, norm_gain.reshape(1, DV), out_weight,
    )
    return pl.pallas_call(
        functools.partial(layer_kernel, n, groups),
        in_specs=[pl.BlockSpec(memory_space=pl.ANY)] * len(inputs),
        out_specs=pl.BlockSpec(memory_space=pltpu.VMEM),
        out_shape=jax.ShapeDtypeStruct((rows, model), bf16),
        scratch_shapes=[pltpu.VMEM(array.shape, array.dtype) for array in inputs] + [
            pltpu.VMEM((heads, DK, DK + DV), bf16),
            pltpu.VMEM((tokens, features), bf16),
            pltpu.VMEM((tokens, features), f32),
            pltpu.VMEM((tokens, features), f32),
            pltpu.VMEM((2, 128, tokens), f32),
            pltpu.VMEM((queries.shape[1] // DK, DK, tokens), bf16),
            pltpu.VMEM((heads, tokens, tokens), bf16),
            pltpu.VMEM((heads, tokens, DK + DV), bf16),
            pltpu.VMEM((n, DK, DK + DV), bf16),
            pltpu.VMEM((n, DK, DV), bf16),
            pltpu.VMEM((heads, DK, DV), bf16),
            pltpu.VMEM((tokens, features), bf16),
            piece, piece, piece, piece, piece,
            dma((len(inputs),)), dma((heads,)), dma((n,)), dma((n,)), dma((heads,)),
            dma((chunks, groups)), dma((chunks, groups)), dma((chunks, groups)), dma((chunks, groups)),
        ],
        compiler_params=pltpu.CompilerParams(
            collective_id=0, has_side_effects=True, vmem_limit_bytes=56 * 2**20
        ),
    )(*inputs)


def solution(mesh):
    placed = (
        P("ctx", "tp"),
        P("ctx", "tp"),
        P("ctx", "tp"),
        P("ctx", "tp"),
        P("ctx", "tp"),
        P("ctx", "tp"),
        P(),
        P("tp", None),
    )
    body = functools.partial(local, mesh.shape["ctx"], mesh.shape["tp"])
    return jax.shard_map(
        body, mesh=mesh, in_specs=placed, out_specs=P(("ctx", "tp"), None), check_vma=False
    )
```

```python
import functools

import jax
import jax.numpy as jnp
from jax import lax
from jax.experimental import pallas as pl
from jax.experimental.pallas import tpu as pltpu
from jax.sharding import PartitionSpec as P

DK = 128
DV = 128
MESH = pl.DeviceIdType.MESH
f32, bf16 = jnp.float32, jnp.bfloat16


def mm(left, right):
    return jnp.dot(left, right, preferred_element_type=f32)


def mm_rows(left, right):
    return lax.dot_general(left, right, (((1,), (1,)), ((), ())), preferred_element_type=f32)


def mm_cols(left, right):
    return lax.dot_general(left, right, (((0,), (0,)), ((), ())), preferred_element_type=f32)


def unit_lower_inverses(lowers):
    size = lowers[0].shape[0]
    row = lax.broadcasted_iota(jnp.int32, (size, size), 0)
    col = lax.broadcasted_iota(jnp.int32, (size, size), 1)
    apart = row ^ col
    eye = jnp.where(row == col, 1.0, 0.0)
    inverses = [eye - jnp.where(apart == 1, lower, 0.0) for lower in lowers]
    step = 2
    while step < size:
        coupling = (apart >= step) & (apart < 2 * step)
        rounded = [inverse.astype(bf16) for inverse in inverses]
        inner = [
            mm(jnp.where(coupling, lower, 0.0).astype(bf16), r).astype(bf16)
            for lower, r in zip(lowers, rounded)
        ]
        inverses = [inverse - mm(r, i) for inverse, r, i in zip(inverses, rounded, inner)]
        step *= 2
    rounded = [inverse.astype(bf16) for inverse in inverses]
    highs = [lower.astype(bf16) for lower in lowers]
    lows = [(lower - high.astype(f32)).astype(bf16) for lower, high in zip(lowers, highs)]
    residuals = [
        (eye - r.astype(f32) - mm(high, r) - mm(low, r)).astype(bf16)
        for high, low, r in zip(highs, lows, rounded)
    ]
    return [r.astype(f32) + mm(r, residual) for r, residual in zip(rounded, residuals)]


def square_sums(source, key_heads, sharing):
    lane = lax.broadcasted_iota(jnp.int32, (DK, 128), 1)
    sums = 0.0
    for group in range(key_heads):
        mine = (lane >= group * sharing) & (lane < (group + 1) * sharing)
        chosen = jnp.where(mine, 1.0, 0.0).astype(bf16)
        values = source[:, group * DK : (group + 1) * DK].astype(f32)
        squares = values * values
        high = squares.astype(bf16)
        sums = sums + mm(high, chosen) + mm((squares - high.astype(f32)).astype(bf16), chosen)
    return sums


def prepare(key_heads, sharing, q_ref, k_ref, rate_ref, decay_ref, turn_ref, scores_ref):
    tokens, heads = q_ref.shape[0], rate_ref.shape[0]
    half = tokens // 2
    row = lax.broadcasted_iota(jnp.int32, (tokens, tokens), 0)
    col = lax.broadcasted_iota(jnp.int32, (tokens, tokens), 1)
    upper = jnp.where(row <= col, 1.0, 0.0)
    total_rows = jnp.dot(
        decay_ref[...], upper, precision=lax.Precision.HIGHEST, preferred_element_type=f32
    )
    rate_rows = rate_ref[...]
    turn_ref[...] = jnp.zeros_like(turn_ref)
    turn_ref[0, :heads] = rate_rows
    turn_ref[1, :heads] = total_rows
    rate, total = turn_ref[0].T, turn_ref[1].T
    key_scale = lax.rsqrt(square_sums(k_ref, key_heads, sharing) + 1e-06)
    query_scale = lax.rsqrt(square_sums(q_ref, key_heads, sharing) + 1e-06)
    key_rows = key_scale.T[:heads]
    erase_rows = rate_rows * jnp.exp(total_rows) * key_rows
    closing = total[tokens - 1 :, :]
    fade = jnp.exp(closing)
    write_scale = jnp.exp(closing - total) * key_scale
    strength = rate * key_scale

    half_row = lax.broadcasted_iota(jnp.int32, (half, half), 0)
    half_col = lax.broadcasted_iota(jnp.int32, (half, half), 1)
    inclusive, strict = half_row >= half_col, half_row > half_col
    parts = []
    for group in range(key_heads):
        key_place = slice(group * DK, (group + 1) * DK)
        queries, keys = q_ref[:, key_place], k_ref[:, key_place]
        gram = mm_rows(keys, keys)
        reads = mm_rows(queries, keys)
        for head in range(group * sharing, (group + 1) * sharing):
            here = slice(head, head + 1)
            total_row, key_row = total_rows[here], key_rows[here]

            def spread(rows, cols):
                return jnp.exp(total[rows, here] - total_row[:, cols])

            top, low = slice(0, half), slice(half, tokens)
            ratio_a = jnp.where(inclusive, spread(top, top), 0.0) * key_row[:, top]
            ratio_b = jnp.where(inclusive, spread(low, low), 0.0) * key_row[:, low]
            ratio_c = spread(low, top) * key_row[:, top]
            scores_ref[head, :half, :half] = (reads[top, top] * ratio_a).astype(bf16)
            scores_ref[head, half:, :half] = (reads[low, top] * ratio_c).astype(bf16)
            scores_ref[head, half:, half:] = (reads[low, low] * ratio_b).astype(bf16)
            lower_a = jnp.where(strict, gram[top, top] * ratio_a * strength[top, here], 0.0)
            lower_b = jnp.where(strict, gram[low, low] * ratio_b * strength[low, here], 0.0)
            lower_c = (gram[low, top] * ratio_c * strength[low, here]).astype(bf16)
            parts.append((
                rate_rows[here], erase_rows[here], write_scale[:, here], fade[:, here],
                jnp.exp(total[:, here]), query_scale[:, here], lower_a, lower_b, lower_c,
            ))
    return parts


def invert(parts):
    inverses = unit_lower_inverses([block for part in parts for block in part[6:8]])
    firsts, seconds = inverses[0::2], inverses[1::2]
    inner = [mm(part[8], first.astype(bf16)).astype(bf16) for part, first in zip(parts, firsts)]
    corners = [-mm(second.astype(bf16), i) for second, i in zip(seconds, inner)]
    return list(zip(firsts, seconds, corners))


def head_map(part, blocks, keys, values, map_ref, both_ref):
    rate_row, erase_row, write_scale, fade = part[:4]
    first, second, corner = blocks
    half = first.shape[0]
    key_row = lax.broadcasted_iota(jnp.int32, (DK, DK), 0)
    key_col = lax.broadcasted_iota(jnp.int32, (DK, DK), 1)

    def solved(scale_row, right):
        left_scale, right_scale = scale_row[:, :half], scale_row[:, half:]
        top = mm((first * left_scale).astype(bf16), right[:half])
        bottom = mm((corner * left_scale).astype(bf16), right[:half])
        bottom += mm((second * right_scale).astype(bf16), right[half:])
        return jnp.concatenate([top, bottom], axis=0)

    both = jnp.concatenate([solved(erase_row, keys), solved(rate_row, values)], axis=1)
    both_ref[...] = both.astype(bf16)
    summary = mm_cols(keys, (both * write_scale).astype(bf16))
    moved = jnp.where(key_row == key_col, fade, 0.0) - summary[:, :DK]
    map_ref[:, :DK] = moved.astype(bf16)
    map_ref[:, DK:] = summary[:, DK:].astype(bf16)


def layer_kernel(
    n, groups, q_hbm, k_hbm, v_hbm, gate_hbm, rate_hbm, decay_hbm, gain_hbm, weight_hbm, out_ref,
    q_ref, k_ref, v_ref, gate_ref, rate_ref, decay_ref, gain_ref, weight,
    map_ref, read_ref, own_ref, gating, turn_ref, scores_ref, both_ref,
    arrived, leaving, state, normed, part, out_r, out_l, in_r, in_l,
    load_sem, map_send, map_recv, state_send, state_recv,
    send_r, recv_r, send_l, recv_l,
):
    heads = map_ref.shape[0]
    apart = n // heads
    chunks, _, rows, width = part.shape
    me, spot = lax.axis_index("ctx"), lax.axis_index("tp")
    my_head = me // apart
    owner = lax.rem(me, apart) == 0

    loads = [
        pltpu.make_async_copy(source, target, load_sem.at[i])
        for i, (source, target) in enumerate((
            (k_hbm, k_ref), (q_hbm, q_ref), (rate_hbm, rate_ref), (decay_hbm, decay_ref),
            (v_hbm, v_ref), (gain_hbm, gain_ref), (gate_hbm, gate_ref), (weight_hbm, weight),
        ))
    ]
    for load in loads[:4]:
        load.start()

    barrier = pltpu.get_barrier_semaphore()
    for other in range(n):
        @pl.when(me != other)
        def _():
            pl.semaphore_signal(barrier, inc=1, device_id={"ctx": other}, device_id_type=MESH)

    after, before = lax.rem(spot + 1, groups), lax.rem(spot + groups - 1, groups)

    @pl.when(spot > 0)
    def _():
        pl.semaphore_signal(barrier, inc=1, device_id={"tp": before}, device_id_type=MESH)

    @pl.when(spot < groups - 1)
    def _():
        pl.semaphore_signal(barrier, inc=1, device_id={"tp": after}, device_id_type=MESH)

    peers = (spot > 0).astype(jnp.int32) + (spot < groups - 1).astype(jnp.int32)
    def map_copy(head, slot, target):
        return pltpu.make_async_remote_copy(
            src_ref=map_ref.at[head], dst_ref=arrived.at[slot],
            send_sem=map_send.at[head], recv_sem=map_recv.at[slot],
            device_id={"ctx": target}, device_id_type=MESH,
        )

    key_heads = k_ref.shape[1] // DK
    sharing = heads // key_heads
    for load in loads[:4]:
        load.wait()
    for load in loads[4:]:
        load.start()
    parts = prepare(key_heads, sharing, q_ref, k_ref, rate_ref, decay_ref, turn_ref, scores_ref)
    blocks = invert(parts)
    loads[4].wait()
    for head in range(heads):
        place = slice(head * DV, (head + 1) * DV)
        group = head // sharing
        keys = k_ref[:, group * DK : (group + 1) * DK]
        head_map(
            parts[head], blocks[head], keys, v_ref[:, place], map_ref.at[head], both_ref.at[head]
        )
        if head == 0:
            pl.semaphore_wait(barrier, n - 1 + peers)

        @pl.when((me != head * apart) & (me < n - 1))
        def _():
            map_copy(head, me, head * apart).start()

    half = q_ref.shape[0] // 2

    def own_part(chosen):
        for head in chosen:
            place = slice(head * DV, (head + 1) * DV)
            group = head // sharing
            queries = q_ref[:, group * DK : (group + 1) * DK].astype(f32)
            decayed, query_scale = parts[head][4:6]
            top = mm(scores_ref[head, :half, :half], both_ref[head, :half])
            low = mm(scores_ref[head, half:], both_ref[head])
            seen = jnp.concatenate([top, low], axis=0)
            read_ref[:, place] = ((decayed * queries - seen[:, :DK]) * query_scale).astype(bf16)
            own_ref[:, place] = seen[:, DK:] * query_scale

    own_part(range(heads // 2))
    for load in loads[5:]:
        load.wait()
    gain = gain_ref[...]
    for head in range(heads):
        place = slice(head * DV, (head + 1) * DV)
        gate = gate_ref[:, place].astype(f32)
        gating[:, place] = gain * (gate / (1.0 + jnp.exp(-gate)))

    def state_copy(head, target):
        return pltpu.make_async_remote_copy(
            src_ref=leaving.at[target], dst_ref=state.at[head],
            send_sem=state_send.at[target], recv_sem=state_recv.at[head],
            device_id={"ctx": target}, device_id_type=MESH,
        )

    @pl.when(me == 0)
    def _():
        state[...] = jnp.zeros_like(state)

    @pl.when(owner)
    def _():
        arrived[pl.ds(me, 1)] = map_ref[pl.ds(my_head, 1)]
        for step in range(n - 1):
            @pl.when(me != step)
            def _():
                map_copy(0, step, step).wait_recv()

        current = arrived[0, :, DK:].astype(f32)
        for step in range(n - 1):
            if step > 0:
                high = current.astype(bf16)
                low = (current - high.astype(f32)).astype(bf16)
                turned = mm(arrived[step, :, :DK], jnp.concatenate([high, low], axis=1))
                current = turned[:, :DV] + turned[:, DV:] + arrived[step, :, DK:].astype(f32)
            leaving[step + 1] = current.astype(bf16)

            @pl.when(me != step + 1)
            def _():
                state_copy(my_head, step + 1).start()

        @pl.when(me > 0)
        def _():
            state[pl.ds(my_head, 1)] = leaving[pl.ds(me, 1)]

    own_part(range(heads // 2, heads))
    for head in range(heads):
        @pl.when((me > 0) & (me != head * apart))
        def _():
            state_copy(head, 0).wait_recv()

    ones = jnp.ones((DV, DV), bf16)
    for head in range(heads):
        place = slice(head * DV, (head + 1) * DV)
        core = mm(read_ref[:, place], state[head]) + own_ref[:, place]
        square_mean = mm((core * core).astype(bf16), ones) * (1.0 / DV)
        normed[:, place] = (core * lax.rsqrt(square_mean + 1e-06) * gating[:, place]).astype(bf16)

    def right_copy(source, c, target):
        return pltpu.make_async_remote_copy(
            src_ref=source.at[c, target], dst_ref=in_r.at[c, target],
            send_sem=send_r.at[c, target], recv_sem=recv_r.at[c, target],
            device_id={"tp": after}, device_id_type=MESH,
        )

    def left_copy(source, c, target):
        return pltpu.make_async_remote_copy(
            src_ref=source.at[c, target], dst_ref=in_l.at[c, target],
            send_sem=send_l.at[c, target], recv_sem=recv_l.at[c, target],
            device_id={"tp": before}, device_id_type=MESH,
        )

    @pl.when(spot == 0)
    def _():
        in_r[:, 0] = jnp.zeros_like(in_r[:, 0])

    @pl.when(spot == groups - 1)
    def _():
        in_l[:, groups - 1] = jnp.zeros_like(in_l[:, groups - 1])

    units = (groups - 1) * chunks

    def right_unit(u):
        return u % chunks, groups - 1 - u // chunks

    def left_unit(u):
        return u % chunks, u // chunks

    for c in range(chunks):
        product = mm(normed[...], weight[:, c * width : (c + 1) * width]).astype(bf16)
        part[c] = product.reshape(groups, rows, width)

        @pl.when(spot == 0)
        def _():
            right_copy(part, *right_unit(c)).start()

        @pl.when(spot == groups - 1)
        def _():
            left_copy(part, *left_unit(c)).start()

    @pl.when(spot == 0)
    def _():
        for u in range(chunks, units):
            right_copy(part, *right_unit(u - chunks)).wait_send()
            right_copy(part, *right_unit(u)).start()

    @pl.when(spot == groups - 1)
    def _():
        for u in range(chunks, units):
            left_copy(part, *left_unit(u - chunks)).wait_send()
            left_copy(part, *left_unit(u)).start()

    lag = 2

    def relay(time, carry):
        u = time - lag * (spot - 1)
        c, target = u % chunks, groups - 1 - u // chunks

        @pl.when((spot > 0) & (u >= 0) & (target > spot))
        def _():
            right_copy(part, c, target).wait_recv()
            out_r[c, target] = (in_r[c, target].astype(f32) + part[c, target].astype(f32)).astype(bf16)
            right_copy(out_r, c, target).start()

        v = time - lag * (groups - 2 - spot)
        d, goal = v % chunks, v // chunks

        @pl.when((spot < groups - 1) & (v >= 0) & (goal < spot))
        def _():
            left_copy(part, d, goal).wait_recv()
            out_l[d, goal] = (in_l[d, goal].astype(f32) + part[d, goal].astype(f32)).astype(bf16)
            left_copy(out_l, d, goal).start()

        return carry

    lax.fori_loop(0, units + lag * (groups - 2), relay, 0)

    for c in range(chunks):
        @pl.when(spot > 0)
        def _():
            right_copy(part, c, spot).wait_recv()

        @pl.when(spot < groups - 1)
        def _():
            left_copy(part, c, spot).wait_recv()

        mixed = part[c, spot].astype(f32) + in_r[c, spot].astype(f32) + in_l[c, spot].astype(f32)
        out_ref[:, c * width : (c + 1) * width] = mixed.astype(bf16)

    for head in range(heads):
        @pl.when((me != head * apart) & (me < n - 1))
        def _():
            map_copy(head, me, head * apart).wait_send()

    for target in range(1, n):
        @pl.when(owner & (me != target))
        def _():
            state_copy(my_head, target).wait_send()

    for c in range(chunks):
        def drain(target, carry):
            @pl.when((target > spot) & (spot > 0))
            def _():
                right_copy(part, c, target).wait_send()

            @pl.when((target < spot) & (spot < groups - 1))
            def _():
                left_copy(part, c, target).wait_send()

            return carry

        lax.fori_loop(0, groups, drain, 0)

    @pl.when(spot == 0)
    def _():
        for u in range(units - chunks, units):
            right_copy(part, *right_unit(u)).wait_send()

    @pl.when(spot == groups - 1)
    def _():
        for u in range(units - chunks, units):
            left_copy(part, *left_unit(u)).wait_send()


def local(n, groups, queries, key_vectors, value_vectors, output_gate, write_rate, log_decay, norm_gain, out_weight):
    tokens = queries.shape[0]
    heads = value_vectors.shape[1] // DV
    features, model = out_weight.shape
    rows = tokens // groups
    chunks = 4
    width = model // chunks
    piece = pltpu.VMEM((chunks, groups, rows, width), bf16)
    dma = pltpu.SemaphoreType.DMA
    inputs = (
        queries, key_vectors, value_vectors, output_gate,
        write_rate.T, log_decay.T, norm_gain.reshape(1, DV), out_weight,
    )
    return pl.pallas_call(
        functools.partial(layer_kernel, n, groups),
        in_specs=[pl.BlockSpec(memory_space=pl.ANY)] * len(inputs),
        out_specs=pl.BlockSpec(memory_space=pltpu.VMEM),
        out_shape=jax.ShapeDtypeStruct((rows, model), bf16),
        scratch_shapes=[pltpu.VMEM(array.shape, array.dtype) for array in inputs] + [
            pltpu.VMEM((heads, DK, DK + DV), bf16),
            pltpu.VMEM((tokens, features), bf16),
            pltpu.VMEM((tokens, features), f32),
            pltpu.VMEM((tokens, features), f32),
            pltpu.VMEM((2, 128, tokens), f32),
            pltpu.VMEM((heads, tokens, tokens), bf16),
            pltpu.VMEM((heads, tokens, DK + DV), bf16),
            pltpu.VMEM((n, DK, DK + DV), bf16),
            pltpu.VMEM((n, DK, DV), bf16),
            pltpu.VMEM((heads, DK, DV), bf16),
            pltpu.VMEM((tokens, features), bf16),
            piece, piece, piece, piece, piece,
            dma((len(inputs),)), dma((heads,)), dma((n,)), dma((n,)), dma((heads,)),
            dma((chunks, groups)), dma((chunks, groups)), dma((chunks, groups)), dma((chunks, groups)),
        ],
        compiler_params=pltpu.CompilerParams(
            collective_id=0, has_side_effects=True, vmem_limit_bytes=56 * 2**20
        ),
    )(*inputs)


def solution(mesh):
    placed = (
        P("ctx", "tp"),
        P("ctx", "tp"),
        P("ctx", "tp"),
        P("ctx", "tp"),
        P("ctx", "tp"),
        P("ctx", "tp"),
        P(),
        P("tp", None),
    )
    body = functools.partial(local, mesh.shape["ctx"], mesh.shape["tp"])
    return jax.shard_map(
        body, mesh=mesh, in_specs=placed, out_specs=P(("ctx", "tp"), None), check_vma=False
    )
```
